128 devices in a mesh: blk: 16 (over x, z), grp: 8 (over y, core).
Axes of the slice: x: 4, y: 4, z: 4, core: 2. Of those that a mesh axis runs over, the one named last changes fastest.
Arguments:
- snapshots: bfloat16 [262144, 1024], P(('grp', 'blk')), may hold values from -1200 to 1200
- start: float32 [1024, 256], replicated, may hold values from -6 to 6
- pivot_dev: int32 [32], replicated, may hold values from 0 to 127, as said below
- pivot_row: int32 [32], replicated, may hold values from 0 to 2047, as said below
Outputs:
- modes: bfloat16 [262144, 256], P(('grp', 'blk'))
- scores: float32 [262144], P(('grp', 'blk'))
- panel_basis: float32 [256, 32], replicated
The draws below stay inside these ranges and needn't reach their ends.
Inputs may be any that keep to these rules, and one draw needn't show every extreme that they name: Together with pivot_row, names 32 distinct global rows pivot_dev * 2048 + pivot_row; the first and the last global row are always among them. `pivot_row`: see pivot_dev.
All inputs are finite; a program needn't handle non-finite values.
Results may differ from the reference program's by a relative error of at most 0.0051.
Values sent between devices are 32-bit elements; how exact they have to be, the bound alone decides.
A program may use at most 64 MiB of HBM per device.

```python
import math
import jax
import jax.numpy as jnp
from jax import lax

ROWS_DEV = 2048
SNAP = 1024
RANK = 256
PANEL = 32
ITERS = 4
ROWS = 262144


def draw_snapshots(key, part):
    keys = jax.random.split(jax.random.fold_in(key, 11), 3)
    positions = jnp.arange(ROWS, dtype=jnp.float32)[:, None]
    row_scale = jnp.exp(jax.random.uniform(keys[0], (ROWS, 1), jnp.float32) * math.log(10.0))
    row_scale = row_scale * jnp.exp(math.log(3.0) * positions / ROWS)
    col_scale = jnp.exp(jax.random.uniform(keys[1], (1, SNAP), jnp.float32) * math.log(10.0))
    values = jnp.clip(jax.random.normal(keys[2], (ROWS, SNAP), jnp.float32), -4.0, 4.0)
    return (values * row_scale * col_scale).astype(jnp.bfloat16)


def pivot_pairs(key):
    keys = jax.random.split(jax.random.fold_in(key, 7), 2)
    middle = jax.random.permutation(keys[0], ROWS - 2)[:PANEL - 2].astype(jnp.int32) + 1
    chosen = jnp.concatenate([jnp.array([0, ROWS - 1], jnp.int32), middle])
    chosen = chosen[jax.random.permutation(keys[1], PANEL)]
    return (chosen // ROWS_DEV, chosen % ROWS_DEV)


def draw_pivot_dev(key, part):
    return pivot_pairs(key)[0].astype(jnp.int32)


def draw_pivot_row(key, part):
    return pivot_pairs(key)[1].astype(jnp.int32)


def gaussian(rng, extent, deviation, reach, kind=jnp.bfloat16):
    result = deviation * jax.random.normal(rng, extent, jnp.float32)
    return jnp.clip(result, min=-reach, max=reach).astype(kind)


def setup_inputs(seed: int = 0) -> dict:
    splits = jax.random.split(jax.random.key(seed), 5)
    return {
        "snapshots": draw_snapshots(jax.random.fold_in(splits[4], 71), 0),
        "start": gaussian(splits[1], (SNAP, RANK), 1.0, 6.0, jnp.float32),
        "pivot_dev": draw_pivot_dev(jax.random.fold_in(splits[4], 71), 0),
        "pivot_row": draw_pivot_row(jax.random.fold_in(splits[4], 71), 0),
    }


def right_solve(factor, matrix):
    return lax.linalg.triangular_solve(factor, matrix, left_side=False, lower=True, transpose_a=True)

def reference(snapshots, start, pivot_dev, pivot_row):
    blocks = snapshots.reshape(ROWS // ROWS_DEV, ROWS_DEV, SNAP)

    def add_block(total, block_rows):
        term = lax.dot_general(block_rows.astype(jnp.float32), block_rows.astype(jnp.float32), (((0,), (0,)), ((), ())), preferred_element_type=jnp.float32)
        return (total + term, None)
    gram_full, unused = lax.scan(add_block, jnp.zeros((SNAP, SNAP), jnp.float32), blocks)
    iterate = start
    for repeat in range(ITERS):
        image = jnp.dot(gram_full, iterate, precision=lax.Precision.HIGHEST)
        square = jnp.dot(image.T, image, precision=lax.Precision.HIGHEST)
        iterate = right_solve(jnp.linalg.cholesky(square), image)
    image = jnp.dot(gram_full, iterate, precision=lax.Precision.HIGHEST)
    small_gram = jnp.dot(iterate.T, image, precision=lax.Precision.HIGHEST) / ROWS
    coef = right_solve(jnp.linalg.cholesky(small_gram), iterate).astype(jnp.bfloat16)
    basis = jnp.dot(snapshots.astype(jnp.float32), coef.astype(jnp.float32), preferred_element_type=jnp.float32)
    global_rows = (pivot_dev * ROWS_DEV + pivot_row).astype(jnp.int32)
    panel = basis[global_rows]
    panel_gram = jnp.dot(panel, panel.T, precision=lax.Precision.HIGHEST)
    panel_basis = right_solve(jnp.linalg.cholesky(panel_gram), panel.T)
    coeffs = jnp.dot(basis, panel_basis, precision=lax.Precision.HIGHEST)
    remaining = basis - jnp.dot(coeffs, panel_basis.T, precision=lax.Precision.HIGHEST)
    scores = jnp.sum(remaining * remaining, axis=1) / RANK
    return (basis.astype(jnp.bfloat16), scores, panel_basis)
```

```python
import functools
import jax, jax.numpy as jnp
from jax import lax
from jax.experimental import pallas as pl
from jax.experimental.pallas import tpu as pltpu
from jax.sharding import Mesh
from jax.sharding import PartitionSpec as P

MESH = pl.DeviceIdType.MESH
F32, BF16 = jnp.float32, jnp.bfloat16
NB = 64
NJ = 4
PAIRS = [(0, 0), (0, 1), (0, 2), (0, 3), (1, 1), (1, 2), (1, 3), (2, 2), (2, 3), (3, 3)]

NN = (((1,), (0,)), ((), ()))
NT = (((1,), (1,)), ((), ()))


def split(x):
    hi = x.astype(BF16)
    return hi, (x - hi.astype(F32)).astype(BF16)


def dot(a, b, dims):
    return lax.dot_general(a, b, dims, preferred_element_type=F32)


def dot3(a, b, dims):
    return dot(a[0], b[0], dims) + (dot(a[0], b[1], dims) + dot(a[1], b[0], dims))


AXES = ("x", "z", "y", "core")
TURNS = (("x", "y", "z"), ("y", "z", "x"), ("z", "x", "y"))


def reduce_kernel(x_ref, pdev_ref, prow_ref, out_ref, loc, r0, acc, r1, a1, r2, a2, r3,
                  send0, recv0, send_down, recv_down, send_up, recv_up, send4, recv4):
    at = {name: lax.axis_index(name) for name in AXES}
    core = at["core"]
    other = 1 - core

    barrier = pltpu.get_barrier_semaphore()
    pl.semaphore_signal(barrier, inc=1, device_id={"core": other}, device_id_type=MESH)
    for axis in ("x", "y", "z"):
        for d in (1, 2, 3):
            pl.semaphore_signal(barrier, inc=1, device_id={axis: lax.rem(at[axis] + d, 4)}, device_id_type=MESH)
    pl.semaphore_wait(barrier, 10)

    def remote(src, dst, send, recv, axis, position):
        return pltpu.make_async_remote_copy(src_ref=src, dst_ref=dst, send_sem=send, recv_sem=recv,
                                            device_id={axis: position}, device_id_type=MESH)

    sent = []

    def go(copy):
        copy.start()
        sent.append(copy)
        return copy

    swaps = {}

    def pair(m):
        for half in (0, 1):
            n = 2 * m + half
            if n < 10:
                i, j = PAIRS[n]
                loc[m, half] = lax.dot_general(x_ref[:, 256 * i:256 * i + 256], x_ref[:, 256 * j:256 * j + 256],
                                               (((0,), (0,)), ((), ())), preferred_element_type=F32)
            elif n == 10:
                me = ((at["y"] * 2 + core) * 4 + at["x"]) * 4 + at["z"]
                where = lax.broadcasted_iota(jnp.int32, (32, 2048), 1)
                hit = (where == prow_ref[...]) & (pdev_ref[...] == me)
                picked = dot(hit.astype(F32).astype(BF16), x_ref[...], NN)
                for part in range(4):
                    loc[m, half, 32 * part:32 * part + 32, :] = picked[:, 256 * part:256 * part + 256]
                loc[m, half, 128:256, :] = jnp.zeros((128, 256), F32)
            else:
                loc[m, half] = jnp.zeros((256, 256), F32)
        swaps[m] = go(remote(loc.at[m, other], r0.at[m], send0.at[m], recv0.at[m], "core", other))

    def offsets(axis):
        return [(d, lax.rem(at[axis] + d, 4)) for d in (1, 2, 3)]

    down, up = {}, {}

    def down1(c):
        for m in (2 * c, 2 * c + 1):
            swaps[m].wait_recv()
            total = loc[m, core] + r0[m]
            acc[c, 2 * (m % 2)] = total[:128]
            acc[c, 2 * (m % 2) + 1] = total[128:]
        axis = TURNS[c][0]
        down[0, c] = [go(remote(acc.at[c, p], r1.at[c, d - 1], send_down.at[0, c, d - 1], recv_down.at[0, c, d - 1], axis, p))
                      for d, p in offsets(axis)]

    def down2(c):
        for copy in down[0, c]:
            copy.wait_recv()
        total = (acc[c, at[TURNS[c][0]]] + r1[c, 0]) + (r1[c, 1] + r1[c, 2])
        for i in range(4):
            a1[c, i] = total[32 * i:32 * i + 32]
        axis = TURNS[c][1]
        down[1, c] = [go(remote(a1.at[c, p], r2.at[c, d - 1], send_down.at[1, c, d - 1], recv_down.at[1, c, d - 1], axis, p))
                      for d, p in offsets(axis)]

    def down3(c):
        for copy in down[1, c]:
            copy.wait_recv()
        total = (a1[c, at[TURNS[c][1]]] + r2[c, 0]) + (r2[c, 1] + r2[c, 2])
        for i in range(4):
            a2[c, i] = total[8 * i:8 * i + 8]
        axis = TURNS[c][2]
        down[2, c] = [go(remote(a2.at[c, p], r3.at[c, d - 1], send_down.at[2, c, d - 1], recv_down.at[2, c, d - 1], axis, p))
                      for d, p in offsets(axis)]

    def up3(c):
        for copy in down[2, c]:
            copy.wait_recv()
        one, two, three = (at[name] for name in TURNS[c])
        out_ref[core, c, one, two, three] = (a2[c, three] + r3[c, 0]) + (r3[c, 1] + r3[c, 2])
        mine = out_ref.at[core, c, one, two, three]
        axis = TURNS[c][2]
        up[2, c] = [go(remote(mine, mine, send_up.at[2, c, d - 1], recv_up.at[2, c, d - 1], axis, p)) for d, p in offsets(axis)]

    def up2(c):
        for copy in up[2, c]:
            copy.wait_recv()
        one, two, three = (at[name] for name in TURNS[c])
        mine = out_ref.at[core, c, one, two]
        axis = TURNS[c][1]
        up[1, c] = [go(remote(mine, mine, send_up.at[1, c, d - 1], recv_up.at[1, c, d - 1], axis, p)) for d, p in offsets(axis)]

    def up1(c):
        for copy in up[1, c]:
            copy.wait_recv()
        one, two, three = (at[name] for name in TURNS[c])
        mine = out_ref.at[core, c, one]
        axis = TURNS[c][0]
        up[0, c] = [go(remote(mine, mine, send_up.at[0, c, d - 1], recv_up.at[0, c, d - 1], axis, p)) for d, p in offsets(axis)]

    def last(c):
        for copy in up[0, c]:
            copy.wait_recv()
        mine = out_ref.at[core, c]
        up[3, c] = go(remote(mine, mine, send4.at[c], recv4.at[c], "core", other))

    pair(0)
    pair(1)
    pair(2)
    pair(3)
    down1(0)
    pair(4)
    pair(5)
    down1(1)
    down1(2)
    for stage in (down2, down3, up3, up2, up1, last):
        for c in range(3):
            stage(c)
    for c in range(3):
        up[3, c].wait_recv()
    for copy in sent:
        copy.wait_send()


def reduce_call(x, pdev, prow):
    return pl.pallas_call(
        reduce_kernel,
        out_shape=jax.ShapeDtypeStruct((2, 3, 4, 4, 4, 8, 256), F32),
        in_specs=[pl.BlockSpec(memory_space=pltpu.VMEM)] * 3,
        out_specs=pl.BlockSpec(memory_space=pltpu.VMEM),
        scratch_shapes=[
            pltpu.VMEM((6, 2, 256, 256), F32), pltpu.VMEM((6, 256, 256), F32), pltpu.VMEM((3, 4, 128, 256), F32),
            pltpu.VMEM((3, 3, 128, 256), F32), pltpu.VMEM((3, 4, 32, 256), F32),
            pltpu.VMEM((3, 3, 32, 256), F32), pltpu.VMEM((3, 4, 8, 256), F32), pltpu.VMEM((3, 3, 8, 256), F32),
            pltpu.SemaphoreType.DMA((6,)), pltpu.SemaphoreType.DMA((6,)),
            pltpu.SemaphoreType.DMA((3, 3, 3)), pltpu.SemaphoreType.DMA((3, 3, 3)),
            pltpu.SemaphoreType.DMA((3, 3, 3)), pltpu.SemaphoreType.DMA((3, 3, 3)),
            pltpu.SemaphoreType.DMA((3,)), pltpu.SemaphoreType.DMA((3,)),
        ],
        compiler_params=pltpu.CompilerParams(vmem_limit_bytes=48 * 1024 * 1024, collective_id=0, has_side_effects=True),
        name="gram_sum",
    )(x, pdev, prow)


def inverse_factors(s_ref, o_ref, panels, first):
    rows_of = lambda i: pl.ds(8 * i, 8)
    spread = lambda row, c: jnp.broadcast_to(row[:, c:c + 1], (8, 128))
    for p in range(panels):
        rows = [s_ref[rows_of(8 * p + r), :] for r in range(8)]
        e = [[spread(rows[r], first + 8 * p + c) if c >= r else None for c in range(8)] for r in range(8)]
        for r in range(8):
            g = 1.0 / e[r][r]
            o_ref[rows_of(8 * p + r), :] = rows[r] * lax.rsqrt(e[r][r])
            pivot = rows[r] * g
            scaled = [e[r][c] * g if c > r else None for c in range(8)]
            for s in range(8):
                if s == r:
                    continue
                f = e[r][s] if s > r else e[s][r]
                rows[s] = rows[s] - f * pivot
                for c in range(max(s, r + 1), 8):
                    e[s][c] = e[s][c] - f * scaled[c]
            rows[r] = pivot
            e[r] = scaled
        for i in range(8 * (p + 1), 8 * panels):
            row = s_ref[rows_of(i), :]
            total = row
            for r in range(8):
                total = total - spread(row, first + 8 * p + r) * rows[r]
            s_ref[rows_of(i), :] = total


def iterate_kernel(inv_rows, b_ref, start_ref, coef_ref, pb_ref,
                   gh, gl, yh, yl, ah, al, th, tl, wh, wl, s_ref, o_ref):
    for n, (i, j) in enumerate(PAIRS):
        block = b_ref[n % 2, n // 2]
        hi, lo = split(block)
        gh[pl.ds(256 * i, 256), pl.ds(256 * j, 256)] = hi
        gl[pl.ds(256 * i, 256), pl.ds(256 * j, 256)] = lo
        if i != j:
            hi, lo = split(block.T)
            gh[pl.ds(256 * j, 256), pl.ds(256 * i, 256)] = hi
            gl[pl.ds(256 * j, 256), pl.ds(256 * i, 256)] = lo

    def times_gram(hi, lo):
        return dot(hi, gh[...], NN) + (dot(hi, gl[...], NN) + dot(lo, gh[...], NN))

    shi, slo = split(start_ref[...])
    first = split(times_gram(shi, slo))
    yh[0], yl[0] = first
    ah[0], al[0] = first
    th[...] = jnp.zeros_like(th)
    tl[...] = jnp.zeros_like(tl)
    s_ref[...] = jnp.ones_like(s_ref)

    row = lax.broadcasted_iota(jnp.int32, (NB, 256), 0)
    lane = lax.broadcasted_iota(jnp.int32, (NB, 256), 1)
    row2, lane2 = row[:, :128], lane[:, :128]

    def step(t, carry):
        vaug = []
        for j in range(NJ):
            k = t - j
            valid = (k >= 0) & (k <= 4)
            kr = jnp.clip(k, 0, 4)
            here = pl.ds(NB * j, NB)
            a = (ah[kr, here, :], al[kr, here, :])
            y = (yh[kr, here, :], yl[kr, here, :])
            scale = jnp.where(k == 4, inv_rows, 1.0).astype(F32)
            twice = tuple(jnp.concatenate([v, v], axis=0) for v in y)
            d = dot3(a, twice, NT) * scale
            w = a[0].astype(F32) + a[1].astype(F32)
            v = (lane == row + NB * j).astype(F32)
            if j > 0:
                before = pl.ds(0, NB * j)
                m = dot3(a, (yh[kr, before, :], yl[kr, before, :]), NT) * scale
                tri = (th[kr, before, before], tl[kr, before, before])
                low = split(dot3(split(m), tri, NT))
                low2 = tuple(jnp.concatenate([x, x], axis=0) for x in low)
                d = d - dot3(low, low2, NT)
                wide = (th[kr, before, :], tl[kr, before, :])
                coef = dot3(low, wide, NN)
                v = v - coef
                ch, cl = split(coef[:, :NB * j])
                w = w - dot3((ch, cl), (ah[kr, before, :], al[kr, before, :]), NN)
            vaug.append(v)
            wh[here, :], wl[here, :] = split(w)
            eye = (row2 == lane2)
            d = jnp.where(valid, d, (lane2 == row2 + NB).astype(F32))
            s_ref[pl.ds(j, NB, stride=8), :] = jnp.where(lane2 < NB, eye.astype(F32), d)
        z = times_gram(wh[...], wl[...])
        inverse_factors(s_ref, o_ref, 8, NB)
        for j in range(NJ):
            k = t - j
            valid = (k >= 0) & (k <= 4)
            kw = jnp.where(valid, k, 5)
            kn = jnp.where(valid, k + 1, 6)
            here = pl.ds(NB * j, NB)
            inv = split(o_ref[pl.ds(j, NB, stride=8), :][:, :NB])
            th[kw, here, :], tl[kw, here, :] = split(dot3(inv, split(vaug[j]), NN))
            y = split(dot3(inv, split(z[NB * j:NB * (j + 1), :]), NN))
            q = dot3(inv, (wh[here, :], wl[here, :]), NN)
            yh[kn, here, :], yl[kn, here, :] = y
            last = k >= 3
            qh, ql = split(q)
            ah[kn, here, :] = jnp.where(last, qh, y[0])
            al[kn, here, :] = jnp.where(last, ql, y[1])
        return carry

    lax.fori_loop(0, 8, step, 0)
    coef = ah[5]
    coef_ref[...] = coef

    for part in range(4):
        xs = b_ref[0, 5, pl.ds(32 * part, 32), :].astype(BF16)
        term = dot(xs, coef[:, 256 * part:256 * (part + 1)], NT)
        panel = term if part == 0 else panel + term
    ph = split(panel)
    twice = tuple(jnp.concatenate([x, x, x, x], axis=0) for x in ph)
    d = dot3(ph, twice, NT)
    r3 = lax.broadcasted_iota(jnp.int32, (32, 128), 0)
    l3 = lax.broadcasted_iota(jnp.int32, (32, 128), 1)
    s_ref[...] = jnp.ones_like(s_ref)
    s_ref[pl.ds(0, 32, stride=8), :] = jnp.where(l3 < 32, (l3 == r3).astype(F32), d)
    inverse_factors(s_ref, o_ref, 4, 32)
    inv = split(o_ref[pl.ds(0, 32, stride=8), :][:, :32])
    pb_ref[...] = dot3(inv, ph, NN).T


def iterate_call(packed, start_t, inv_rows):
    return pl.pallas_call(
        functools.partial(iterate_kernel, inv_rows),
        out_shape=(jax.ShapeDtypeStruct((256, 1024), BF16), jax.ShapeDtypeStruct((256, 32), F32)),
        in_specs=[pl.BlockSpec(memory_space=pltpu.VMEM)] * 2,
        out_specs=(pl.BlockSpec(memory_space=pltpu.VMEM),) * 2,
        scratch_shapes=[
            pltpu.VMEM((1024, 1024), BF16), pltpu.VMEM((1024, 1024), BF16),
            pltpu.VMEM((7, 256, 1024), BF16), pltpu.VMEM((7, 256, 1024), BF16),
            pltpu.VMEM((7, 256, 1024), BF16), pltpu.VMEM((7, 256, 1024), BF16),
            pltpu.VMEM((6, 256, 256), BF16), pltpu.VMEM((6, 256, 256), BF16),
            pltpu.VMEM((256, 1024), BF16), pltpu.VMEM((256, 1024), BF16),
            pltpu.VMEM((512, 128), F32), pltpu.VMEM((512, 128), F32),
        ],
        compiler_params=pltpu.CompilerParams(vmem_limit_bytes=56 * 1024 * 1024),
        name="iterate",
    )(packed, start_t)


def project_kernel(x_ref, coef_ref, pb_ref, modes_ref, scores_ref, proj_hi, proj_lo):
    @pl.when(pl.program_id(0) == 0)
    def _():
        pb = split(pb_ref[...])
        proj_hi[...], proj_lo[...] = split(dot3(pb, pb, NT))

    basis = dot(x_ref[...], coef_ref[...], NT)
    hi, lo = split(basis)
    modes_ref[...] = hi
    remaining = basis - dot3((hi, lo), (proj_hi[...], proj_lo[...]), NN)
    hi, lo = split(remaining * remaining)
    ones = jnp.ones((8, hi.shape[1]), BF16)
    total = dot(ones, hi, NT) + dot(ones, lo, NT)
    scores_ref[0] = total[:1] * (1.0 / hi.shape[1])


def project_call(x, coef_t, pb):
    rows = 256
    steps = x.shape[0] // rows
    return pl.pallas_call(
        project_kernel,
        grid=(steps,),
        out_shape=(jax.ShapeDtypeStruct((x.shape[0], 256), BF16), jax.ShapeDtypeStruct((steps, 1, rows), F32)),
        in_specs=[pl.BlockSpec((rows, 1024), lambda i: (i, 0)), pl.BlockSpec((256, 1024), lambda i: (0, 0)),
                  pl.BlockSpec((256, 32), lambda i: (0, 0))],
        out_specs=(pl.BlockSpec((rows, 256), lambda i: (i, 0)), pl.BlockSpec((1, 1, rows), lambda i: (i, 0, 0))),
        scratch_shapes=[pltpu.VMEM((256, 256), BF16), pltpu.VMEM((256, 256), BF16)],
        compiler_params=pltpu.CompilerParams(vmem_limit_bytes=32 * 1024 * 1024),
        name="project",
    )(x, coef_t, pb)


def local(snapshots, start, pivot_dev, pivot_row):
    rows_total = snapshots.shape[0] * lax.axis_size(AXES)
    packed = reduce_call(snapshots, pivot_dev[:, None], pivot_row[:, None])
    coef_t, panel_basis = iterate_call(packed.reshape(2, 6, 256, 256), start.T, 1.0 / rows_total)
    modes, scores = project_call(snapshots, coef_t, panel_basis)
    return (modes, scores.reshape(-1), panel_basis)


def solution(mesh):
    torus = Mesh(mesh.devices.reshape(4, 4, 4, 2), AXES)
    rows = ("y", "core", "x", "z")
    return jax.shard_map(
        local,
        mesh=torus,
        in_specs=(P(rows, None), P(), P(), P()),
        out_specs=(P(rows, None), P(rows), P()),
        check_vma=False,
    )
```

```python
import functools
import jax, jax.numpy as jnp
from jax import lax
from jax.experimental import pallas as pl
from jax.experimental.pallas import tpu as pltpu
from jax.sharding import Mesh
from jax.sharding import PartitionSpec as P

MESH = pl.DeviceIdType.MESH
F32, BF16 = jnp.float32, jnp.bfloat16
NB = 64
NJ = 4
PAIRS = [(0, 0), (0, 1), (0, 2), (0, 3), (1, 1), (1, 2), (1, 3), (2, 2), (2, 3), (3, 3)]

NN = (((1,), (0,)), ((), ()))
NT = (((1,), (1,)), ((), ()))


def split(x):
    hi = x.astype(BF16)
    return hi, (x - hi.astype(F32)).astype(BF16)


def dot(a, b, dims):
    return lax.dot_general(a, b, dims, preferred_element_type=F32)


def dot3(a, b, dims):
    return dot(a[0], b[0], dims) + (dot(a[0], b[1], dims) + dot(a[1], b[0], dims))


AXES = ("x", "z", "y", "core")
TURNS = (("x", "y", "z"), ("y", "z", "x"), ("z", "x", "y"))


def reduce_kernel(x_ref, pdev_ref, prow_ref, out_ref, loc, r0, acc, r1, a1, r2, a2, r3,
                  send0, recv0, send_down, recv_down, send_up, recv_up, send4, recv4):
    at = {name: lax.axis_index(name) for name in AXES}
    core = at["core"]
    other = 1 - core

    barrier = pltpu.get_barrier_semaphore()
    pl.semaphore_signal(barrier, inc=1, device_id={"core": other}, device_id_type=MESH)
    for axis in ("x", "y", "z"):
        for d in (1, 2, 3):
            pl.semaphore_signal(barrier, inc=1, device_id={axis: lax.rem(at[axis] + d, 4)}, device_id_type=MESH)
    pl.semaphore_wait(barrier, 10)

    def remote(src, dst, send, recv, axis, position):
        return pltpu.make_async_remote_copy(src_ref=src, dst_ref=dst, send_sem=send, recv_sem=recv,
                                            device_id={axis: position}, device_id_type=MESH)

    sent = []

    def go(copy):
        copy.start()
        sent.append(copy)
        return copy

    swaps = {}

    def pair(m):
        for half in (0, 1):
            n = 2 * m + half
            if n < 10:
                i, j = PAIRS[n]
                loc[m, half] = lax.dot_general(x_ref[:, 256 * i:256 * i + 256], x_ref[:, 256 * j:256 * j + 256],
                                               (((0,), (0,)), ((), ())), preferred_element_type=F32)
            elif n == 10:
                me = ((at["y"] * 2 + core) * 4 + at["x"]) * 4 + at["z"]
                where = lax.broadcasted_iota(jnp.int32, (32, 2048), 1)
                hit = (where == prow_ref[...]) & (pdev_ref[...] == me)
                picked = dot(hit.astype(F32).astype(BF16), x_ref[...], NN)
                for part in range(4):
                    loc[m, half, 32 * part:32 * part + 32, :] = picked[:, 256 * part:256 * part + 256]
                loc[m, half, 128:256, :] = jnp.zeros((128, 256), F32)
            else:
                loc[m, half] = jnp.zeros((256, 256), F32)
        swaps[m] = go(remote(loc.at[m, other], r0.at[m], send0.at[m], recv0.at[m], "core", other))

    def offsets(axis):
        return [(d, lax.rem(at[axis] + d, 4)) for d in (1, 2, 3)]

    down, up = {}, {}

    def down1(c):
        for m in (2 * c, 2 * c + 1):
            swaps[m].wait_recv()
            total = loc[m, core] + r0[m]
            acc[c, 2 * (m % 2)] = total[:128]
            acc[c, 2 * (m % 2) + 1] = total[128:]
        axis = TURNS[c][0]
        down[0, c] = [go(remote(acc.at[c, p], r1.at[c, d - 1], send_down.at[0, c, d - 1], recv_down.at[0, c, d - 1], axis, p))
                      for d, p in offsets(axis)]

    def down2(c):
        for copy in down[0, c]:
            copy.wait_recv()
        total = (acc[c, at[TURNS[c][0]]] + r1[c, 0]) + (r1[c, 1] + r1[c, 2])
        for i in range(4):
            a1[c, i] = total[32 * i:32 * i + 32]
        axis = TURNS[c][1]
        down[1, c] = [go(remote(a1.at[c, p], r2.at[c, d - 1], send_down.at[1, c, d - 1], recv_down.at[1, c, d - 1], axis, p))
                      for d, p in offsets(axis)]

    def down3(c):
        for copy in down[1, c]:
            copy.wait_recv()
        total = (a1[c, at[TURNS[c][1]]] + r2[c, 0]) + (r2[c, 1] + r2[c, 2])
        for i in range(4):
            a2[c, i] = total[8 * i:8 * i + 8]
        axis = TURNS[c][2]
        down[2, c] = [go(remote(a2.at[c, p], r3.at[c, d - 1], send_down.at[2, c, d - 1], recv_down.at[2, c, d - 1], axis, p))
                      for d, p in offsets(axis)]

    def up3(c):
        for copy in down[2, c]:
            copy.wait_recv()
        one, two, three = (at[name] for name in TURNS[c])
        out_ref[core, c, one, two, three] = (a2[c, three] + r3[c, 0]) + (r3[c, 1] + r3[c, 2])
        mine = out_ref.at[core, c, one, two, three]
        axis = TURNS[c][2]
        up[2, c] = [go(remote(mine, mine, send_up.at[2, c, d - 1], recv_up.at[2, c, d - 1], axis, p)) for d, p in offsets(axis)]

    def up2(c):
        for copy in up[2, c]:
            copy.wait_recv()
        one, two, three = (at[name] for name in TURNS[c])
        mine = out_ref.at[core, c, one, two]
        axis = TURNS[c][1]
        up[1, c] = [go(remote(mine, mine, send_up.at[1, c, d - 1], recv_up.at[1, c, d - 1], axis, p)) for d, p in offsets(axis)]

    def up1(c):
        for copy in up[1, c]:
            copy.wait_recv()
        one, two, three = (at[name] for name in TURNS[c])
        mine = out_ref.at[core, c, one]
        axis = TURNS[c][0]
        up[0, c] = [go(remote(mine, mine, send_up.at[0, c, d - 1], recv_up.at[0, c, d - 1], axis, p)) for d, p in offsets(axis)]

    def last(c):
        for copy in up[0, c]:
            copy.wait_recv()
        mine = out_ref.at[core, c]
        up[3, c] = go(remote(mine, mine, send4.at[c], recv4.at[c], "core", other))

    pair(0)
    pair(1)
    pair(2)
    pair(3)
    down1(0)
    pair(4)
    pair(5)
    down1(1)
    down1(2)
    for stage in (down2, down3, up3, up2, up1, last):
        for c in range(3):
            stage(c)
    for c in range(3):
        up[3, c].wait_recv()
    for copy in sent:
        copy.wait_send()


def reduce_call(x, pdev, prow):
    return pl.pallas_call(
        reduce_kernel,
        out_shape=jax.ShapeDtypeStruct((2, 3, 4, 4, 4, 8, 256), F32),
        in_specs=[pl.BlockSpec(memory_space=pltpu.VMEM)] * 3,
        out_specs=pl.BlockSpec(memory_space=pltpu.VMEM),
        scratch_shapes=[
            pltpu.VMEM((6, 2, 256, 256), F32), pltpu.VMEM((6, 256, 256), F32), pltpu.VMEM((3, 4, 128, 256), F32),
            pltpu.VMEM((3, 3, 128, 256), F32), pltpu.VMEM((3, 4, 32, 256), F32),
            pltpu.VMEM((3, 3, 32, 256), F32), pltpu.VMEM((3, 4, 8, 256), F32), pltpu.VMEM((3, 3, 8, 256), F32),
            pltpu.SemaphoreType.DMA((6,)), pltpu.SemaphoreType.DMA((6,)),
            pltpu.SemaphoreType.DMA((3, 3, 3)), pltpu.SemaphoreType.DMA((3, 3, 3)),
            pltpu.SemaphoreType.DMA((3, 3, 3)), pltpu.SemaphoreType.DMA((3, 3, 3)),
            pltpu.SemaphoreType.DMA((3,)), pltpu.SemaphoreType.DMA((3,)),
        ],
        compiler_params=pltpu.CompilerParams(vmem_limit_bytes=48 * 1024 * 1024, collective_id=0, has_side_effects=True),
        name="gram_sum",
    )(x, pdev, prow)


def inverse_factors(augs, panels, first, work=()):
    sub = lax.broadcasted_iota(jnp.int32, (8, 128), 0)
    spread = lambda v, c: jnp.broadcast_to(v[:, c:c + 1], (8, 128))
    one = lambda v, r: jnp.broadcast_to(v[r:r + 1, :], (8, 128))
    every = range(len(augs))
    work, done = list(work), 0
    groups = [[aug[8 * q:8 * q + 8, :] for q in range(panels)] for aug in augs]
    outs = [[] for _ in every]
    late = []

    def columns_of(n, q, p):
        return [spread(groups[n][q], first + 8 * p + c) for c in range(8)]

    def reduce(n, q, columns, lines):
        terms = [columns[r] * lines[r] for r in range(8)]
        while len(terms) > 1:
            terms = [terms[i] + terms[i + 1] for i in range(0, len(terms), 2)]
        groups[n][q] = groups[n][q] - terms[0]

    for p in range(panels):
        v = [groups[n][p] for n in every]
        out = list(v)
        columns = [columns_of(n, p, p) for n in every]
        below = {}
        for r in range(8):
            for n in every:
                here = columns[n][r]
                pivot = one(here, r)
                inverse = 1.0 / pivot
                line = one(v[n], r)
                for c in range(r + 1, 8):
                    value = one(columns[n][c], r) * inverse
                    columns[n][c] = jnp.where(sub == r, value, columns[n][c] - here * value)
                out[n] = jnp.where(sub == r, line * lax.rsqrt(pivot), out[n])
                line = line * inverse
                v[n] = jnp.where(sub == r, line, v[n] - here * line)
            share = -(-len(late) // max(1, 6 - r))
            for n, q, lines in late[:share]:
                reduce(n, q, columns_of(n, q, p - 1), lines)
            late = late[share:]
            if r == 5 and p + 1 < panels:
                assert not late
                below = {n: columns_of(n, p + 1, p) for n in every}
            target = len(work) * (8 * p + r + 1) // (8 * panels)
            while done < target:
                work[done]()
                done += 1
        for n in every:
            outs[n].append(out[n])
            lines = [one(v[n], r) for r in range(8)]
            if p + 1 < panels:
                reduce(n, p + 1, below[n], lines)
            late += [(n, q, lines) for q in range(p + 2, panels)]
        late.sort(key=lambda item: item[1])
    return [jnp.concatenate(o, axis=0) for o in outs]


def iterate_kernel(inv_rows, b_ref, start_ref, x_hbm, modes_hbm, scores_ref, pb_ref,
                   gh, gl, sh, sl, yh, yl, qh, ql, th, tl, wh, wl, zh, zl, zf, x_ref, modes_ref, basis_ref,
                   x_sem, modes_sem):
    load = pltpu.make_async_copy(x_hbm, x_ref, x_sem)
    load.start()
    for n, (i, j) in enumerate(PAIRS):
        block = b_ref[n % 2, n // 2]
        hi, lo = split(block)
        gh[pl.ds(256 * i, 256), pl.ds(256 * j, 256)] = hi
        gl[pl.ds(256 * i, 256), pl.ds(256 * j, 256)] = lo
        if i != j:
            hi, lo = split(block.T)
            gh[pl.ds(256 * j, 256), pl.ds(256 * i, 256)] = hi
            gl[pl.ds(256 * j, 256), pl.ds(256 * i, 256)] = lo
    sh[...], sl[...] = split(start_ref[...].T)

    def times_gram(hi, lo):
        return dot(hi, gh[...], NN) + (dot(hi, gl[...], NN) + dot(lo, gh[...], NN))

    def block(j):
        return pl.ds(NB * j, NB)

    yh[0, block(0), :], yl[0, block(0), :] = split(times_gram(sh[block(0), :], sl[block(0), :]))
    th[...] = jnp.zeros_like(th)
    tl[...] = jnp.zeros_like(tl)

    row = lax.broadcasted_iota(jnp.int32, (NB, 256), 0)
    lane = lax.broadcasted_iota(jnp.int32, (NB, 256), 1)
    eye = (row == lane)[:, :NB].astype(F32)

    def stacked3(a, b, dims):
        n = a[0].shape[0]
        both = dot(jnp.concatenate([a[0], a[1]], axis=0), b[0], dims)
        return both[:n] + both[n:] + dot(a[0], b[1], dims)

    for t in range(8):
        tasks = [(t - j, j) for j in range(NJ) if 0 <= t - j <= 4]
        go = [(k, j) for k, j in tasks if k < 4]
        ahead = t < 3
        ms, ds, lows, vaug, coefs, part = {}, {}, {}, {}, {}, {}

        def left(k, where, lanes=slice(None)):
            return (yh[k, where, lanes], yl[k, where, lanes]) if k < 4 else (qh[where, lanes], ql[where, lanes])

        for k, j in tasks:
            scale = inv_rows if k == 4 else 1.0
            a = left(k, block(j))
            ds[k] = stacked3(a, (yh[k, block(j), :], yl[k, block(j), :]), NT) * scale
            if j > 0:
                before = pl.ds(0, NB * j)
                ms[k] = split(stacked3(a, (yh[k, before, :], yl[k, before, :]), NT) * scale)
        for k, j in tasks:
            if j > 0:
                before = pl.ds(0, NB * j)
                lows[k] = split(stacked3(ms[k], (th[k, before, before], tl[k, before, before]), NT))
        for k, j in tasks:
            if j > 0:
                ds[k] = ds[k] - stacked3(lows[k], lows[k], NT)

        def make_v(k, j):
            v = (lane == row + NB * j).astype(F32)
            if j > 0:
                coef = stacked3(lows[k], (th[k, pl.ds(0, NB * j), :], tl[k, pl.ds(0, NB * j), :]), NN)
                v = v - coef
                coefs[k] = split(coef[:, :NB * j])
            vaug[k] = split(v)

        def make_w(n, k, j, lanes):
            a = left(k, block(j), lanes)
            if j > 0:
                w = a[0].astype(F32) + a[1].astype(F32)
                a = split(w - stacked3(coefs[k], left(k, pl.ds(0, NB * j), lanes), NN))
            wh[block(n), lanes], wl[block(n), lanes] = a

        def make_ahead():
            n = len(go)
            wh[block(n), :], wl[block(n), :] = sh[block(t + 1), :], sl[block(t + 1), :]

        rows = NB * (len(go) + ahead)

        def make_z(lanes, depth, last):
            new = stacked3((wh[:rows, depth], wl[:rows, depth]), (gh[depth, lanes], gl[depth, lanes]), NN)
            part[0] = new if depth.start == 0 else part[0] + new
            if last:
                zh[:rows, lanes], zl[:rows, lanes] = split(part[0])

        work = [functools.partial(make_v, k, j) for k, j in tasks]
        work += [functools.partial(make_w, n, k, j, slice(512 * i, 512 * i + 512))
                 for n, (k, j) in enumerate(go + [task for task in tasks if task not in go]) for i in range(2)]
        if ahead:
            work.append(make_ahead)
        if rows:
            work += [functools.partial(make_z, slice(256 * i, 256 * i + 256), slice(256 * d, 256 * d + 256), d == 3)
                     for i in range(4) for d in range(4)]
        invs = inverse_factors([jnp.concatenate([eye, ds[k]], axis=1) for k, j in tasks], 8, NB, work)
        invs = {k: split(inv[:, :NB]) for (k, j), inv in zip(tasks, invs)}
        for n, (k, j) in enumerate(go):
            yh[k + 1, block(j), :], yl[k + 1, block(j), :] = split(stacked3(invs[k], (zh[block(n), :], zl[block(n), :]), NN))
            if k == 3:
                qh[block(j), :], ql[block(j), :] = split(stacked3(invs[k], (wh[block(n), :], wl[block(n), :]), NN))
        if ahead:
            n = len(go)
            yh[0, block(t + 1), :], yl[0, block(t + 1), :] = zh[block(n), :], zl[block(n), :]
        for k, j in tasks:
            if j < NJ - 1:
                th[k, block(j), :], tl[k, block(j), :] = split(stacked3(invs[k], vaug[k], NN))
            if k == 4:
                n = len(go)
                zf[block(j), :] = stacked3(invs[k], (wh[block(n), :], wl[block(n), :]), NN).astype(BF16)

    coef = zf[...]
    for part in range(4):
        xs = b_ref[0, 5, pl.ds(32 * part, 32), :].astype(BF16)
        term = dot(xs, coef[:, 256 * part:256 * (part + 1)], NT)
        panel = term if part == 0 else panel + term
    ph = split(panel)
    small = jnp.concatenate(
        [eye[:32, :32], dot3(ph, ph, NT), jnp.zeros((32, 64), F32)], axis=1)

    load.wait()
    stores = []
    for n in range(8):
        here = pl.ds(256 * n, 256)
        basis = dot(x_ref[here, :], coef, NT)
        basis_ref[here, :] = basis
        modes_ref[here, :] = basis.astype(BF16)
        stores.append(pltpu.make_async_copy(modes_ref.at[here, :], modes_hbm.at[here, :], modes_sem.at[n]))
        stores[-1].start()

    inv = split(inverse_factors([small], 4, 32)[0][:, :32])
    pbt = dot3(inv, ph, NN)
    pb_ref[...] = pbt.T
    pb = split(pbt.T)
    proj = split(dot3(pb, pb, NT))
    ones = jnp.ones((8, 256), BF16)
    for n in range(8):
        here = pl.ds(256 * n, 256)
        basis = basis_ref[here, :]
        remaining = basis - dot3(split(basis), proj, NN)
        hi, lo = split(remaining * remaining)
        total = dot(ones, hi, NT) + dot(ones, lo, NT)
        scores_ref[n:n + 1, :] = total[:1] * (1.0 / 256)
    for copy in stores:
        copy.wait()


def iterate_call(packed, start, x, inv_rows):
    vmem = lambda: pl.BlockSpec(memory_space=pltpu.VMEM)
    hbm = lambda: pl.BlockSpec(memory_space=pltpu.HBM)
    rows = x.shape[0]
    return pl.pallas_call(
        functools.partial(iterate_kernel, inv_rows),
        out_shape=(jax.ShapeDtypeStruct((rows, 256), BF16), jax.ShapeDtypeStruct((8, 256), F32),
                   jax.ShapeDtypeStruct((256, 32), F32)),
        in_specs=[vmem(), vmem(), hbm()],
        out_specs=(hbm(), vmem(), vmem()),
        scratch_shapes=[
            pltpu.VMEM((1024, 1024), BF16), pltpu.VMEM((1024, 1024), BF16),
            pltpu.VMEM((256, 1024), BF16), pltpu.VMEM((256, 1024), BF16),
            pltpu.VMEM((5, 256, 1024), BF16), pltpu.VMEM((5, 256, 1024), BF16),
            pltpu.VMEM((256, 1024), BF16), pltpu.VMEM((256, 1024), BF16),
            pltpu.VMEM((5, 256, 256), BF16), pltpu.VMEM((5, 256, 256), BF16),
            pltpu.VMEM((256, 1024), BF16), pltpu.VMEM((256, 1024), BF16),
            pltpu.VMEM((256, 1024), BF16), pltpu.VMEM((256, 1024), BF16),
            pltpu.VMEM((256, 1024), BF16),
            pltpu.VMEM((rows, 1024), BF16), pltpu.VMEM((rows, 256), BF16), pltpu.VMEM((rows, 256), F32),
            pltpu.SemaphoreType.DMA, pltpu.SemaphoreType.DMA((8,)),
        ],
        compiler_params=pltpu.CompilerParams(vmem_limit_bytes=56 * 1024 * 1024),
        name="iterate",
    )(packed, start, x)


def local(snapshots, start, pivot_dev, pivot_row):
    rows_total = snapshots.shape[0] * lax.axis_size(AXES)
    packed = reduce_call(snapshots, pivot_dev[:, None], pivot_row[:, None])
    modes, scores, panel_basis = iterate_call(packed.reshape(2, 6, 256, 256), start, snapshots, 1.0 / rows_total)
    return (modes, scores.reshape(-1), panel_basis)


def solution(mesh):
    torus = Mesh(mesh.devices.reshape(4, 4, 4, 2), AXES)
    rows = ("y", "core", "x", "z")
    return jax.shard_map(
        local,
        mesh=torus,
        in_specs=(P(rows, None), P(), P(), P()),
        out_specs=(P(rows, None), P(rows), P()),
        check_vma=False,
    )
```

```python
import functools
import jax, jax.numpy as jnp
from jax import lax
from jax.experimental import pallas as pl
from jax.experimental.pallas import tpu as pltpu
from jax.sharding import Mesh
from jax.sharding import PartitionSpec as P

MESH = pl.DeviceIdType.MESH
F32, BF16 = jnp.float32, jnp.bfloat16
NB = 64
NJ = 4
PAIRS = [(0, 0), (0, 1), (0, 2), (0, 3), (1, 1), (1, 2), (1, 3), (2, 2), (2, 3), (3, 3)]

NN = (((1,), (0,)), ((), ()))
NT = (((1,), (1,)), ((), ()))


def split(x):
    hi = x.astype(BF16)
    return hi, (x - hi.astype(F32)).astype(BF16)


def dot(a, b, dims):
    return lax.dot_general(a, b, dims, preferred_element_type=F32)


def dot3(a, b, dims):
    return dot(a[0], b[0], dims) + (dot(a[0], b[1], dims) + dot(a[1], b[0], dims))


AXES = ("x", "z", "y", "core")
TURNS = (("x", "y", "z"), ("y", "z", "x"), ("z", "x", "y"))


def reduce_kernel(x_hbm, pdev_ref, prow_ref, out_ref, x_ref, loc, r0, acc, r1, a1, r2, x_sem,
                  send0, recv0, send1, recv1, send2, recv2, send3, recv3, send4, recv4, send5, recv5):
    at = {name: lax.axis_index(name) for name in AXES}
    core = at["core"]
    other = 1 - core

    slabs = [pltpu.make_async_copy(x_hbm.at[:, pl.ds(256 * i, 256)], x_ref.at[:, pl.ds(256 * i, 256)], x_sem.at[i])
             for i in range(4)]
    for slab in slabs:
        slab.start()

    def axis_peers(axis):
        return [(d - 1, {axis: lax.rem(at[axis] + d, 4)}) for d in (1, 2, 3)]

    def plane_peers(m):
        one, two = TURNS[m % 3][1:]
        return [(4 * d + e - 1, {one: lax.rem(at[one] + d, 4), two: lax.rem(at[two] + e, 4)})
                for d in range(4) for e in range(4) if d or e]

    barrier = pltpu.get_barrier_semaphore()
    pl.semaphore_signal(barrier, inc=1, device_id={"core": other}, device_id_type=MESH)
    for axis in ("x", "y", "z"):
        for _, peer in axis_peers(axis):
            pl.semaphore_signal(barrier, inc=1, device_id=peer, device_id_type=MESH)
    for c in range(3):
        for slot, peer in plane_peers(c):
            if (slot + 1) // 4 and (slot + 1) % 4:
                pl.semaphore_signal(barrier, inc=1, device_id=peer, device_id_type=MESH)

    sent = []

    def go(src, dst, send, recv, peer):
        copy = pltpu.make_async_remote_copy(src_ref=src, dst_ref=dst, send_sem=send, recv_sem=recv,
                                            device_id=peer, device_id_type=MESH)
        copy.start()
        sent.append(copy)
        return copy

    def keep(m, half, value):
        loc[m, half, 0] = value[:, :128]
        loc[m, half, 1] = value[:, 128:]

    def pair(m):
        for half in (0, 1):
            n = 2 * m + half
            if n < 10:
                i, j = PAIRS[n]
                keep(m, half, lax.dot_general(x_ref[:, 256 * i:256 * i + 256], x_ref[:, 256 * j:256 * j + 256],
                                              (((0,), (0,)), ((), ())), preferred_element_type=F32))
            elif n == 10:
                me = ((at["y"] * 2 + core) * 4 + at["x"]) * 4 + at["z"]
                pivot = lax.broadcasted_iota(jnp.int32, (32, 128), 0)
                lane = lax.broadcasted_iota(jnp.int32, (32, 128), 1)
                target = jnp.full((32, 128), -1, jnp.int32)
                for i in range(32):
                    target = jnp.where(pivot == i, jnp.where(pdev_ref[i] == me, prow_ref[i], -1), target)
                hit = jnp.concatenate([(target == lane + 128 * i).astype(F32).astype(BF16) for i in range(16)], axis=1)
                picked = dot(hit, x_ref[...], NN)
                keep(m, half, jnp.concatenate([picked[:, 256 * part:256 * part + 256] for part in range(4)]
                                              + [jnp.zeros((128, 256), F32)], axis=0))
            else:
                keep(m, half, jnp.zeros((256, 256), F32))

    swaps, down, across, back, up, over = {}, {}, {}, {}, {}, []

    def swap(m):
        swaps[m] = go(loc.at[m, other], r0.at[m], send0.at[m], recv0.at[m], {"core": other})

    def down1(m):
        swaps[m].wait_recv()
        for i in range(2):
            total = loc[m, core, i] + r0[m, i]
            acc[m, 2 * i] = total[:128]
            acc[m, 2 * i + 1] = total[128:]
        axis = TURNS[m % 3][0]
        down[m] = [go(acc.at[m, peer[axis]], r1.at[m, slot], send1.at[m, slot], recv1.at[m, slot], peer)
                   for slot, peer in axis_peers(axis)]

    def down2(m):
        for copy in down[m]:
            copy.wait_recv()
        total = (acc[m, at[TURNS[m % 3][0]]] + r1[m, 0]) + (r1[m, 1] + r1[m, 2])
        for i in range(16):
            a1[m, i // 4, i % 4] = total[8 * i:8 * i + 8]
        one, two = TURNS[m % 3][1:]
        across[m] = [go(a1.at[m, peer[one], peer[two]], r2.at[m, slot], send2.at[m, slot], recv2.at[m, slot], peer)
                     for slot, peer in plane_peers(m)]

    def up2(m):
        for copy in across[m]:
            copy.wait_recv()
        one, two, three = (at[name] for name in TURNS[m % 3])
        terms = [a1[m, two, three]] + [r2[m, slot] for slot in range(15)]
        while len(terms) > 1:
            terms = [terms[i] + terms[i + 1] for i in range(0, len(terms), 2)]
        out_ref[core, m, one, two, three] = terms[0]
        mine = out_ref.at[core, m, one, two, three]
        back[m] = [go(mine, mine, send3.at[m, slot], recv3.at[m, slot], peer) for slot, peer in plane_peers(m)]

    def up1(m):
        for copy in back[m]:
            copy.wait_recv()
        axis = TURNS[m % 3][0]
        mine = out_ref.at[core, m, at[axis]]
        up[m] = [go(mine, mine, send4.at[m, slot], recv4.at[m, slot], peer) for slot, peer in axis_peers(axis)]
        over.append(go(mine, mine, send5.at[m, 3], recv5.at[m, 3], {"core": other}))

    def forward(m, slot):
        up[m][slot].wait_recv()
        piece = out_ref.at[core, m, lax.rem(at[TURNS[m % 3][0]] + 3 - slot, 4)]
        over.append(go(piece, piece, send5.at[m, slot], recv5.at[m, slot], {"core": other}))

    early, late = (0, 1, 2), (3, 4, 5)
    for m in early:
        for slab in slabs[2 * m:2 * m + 2]:
            slab.wait()
        pair(m)
    pl.semaphore_wait(barrier, 37)
    for m in early:
        swap(m)
    pair(3)
    swap(3)
    for m in early:
        down1(m)
    pair(4)
    swap(4)
    pair(5)
    swap(5)
    for stage, units in ((down1, late), (down2, early), (down2, late), (up2, early), (up2, late), (up1, early), (up1, late)):
        for m in units:
            stage(m)
    for units in (early, late):
        for slot in (0, 2, 1):
            for m in units:
                forward(m, slot)
    for copy in over:
        copy.wait_recv()
    for copy in sent:
        copy.wait_send()


def reduce_call(x, pdev, prow):
    dma = pltpu.SemaphoreType.DMA
    return pl.pallas_call(
        reduce_kernel,
        out_shape=jax.ShapeDtypeStruct((2, 6, 4, 4, 4, 8, 128), F32),
        in_specs=[pl.BlockSpec(memory_space=pltpu.HBM)] + [pl.BlockSpec(memory_space=pltpu.SMEM)] * 2,
        out_specs=pl.BlockSpec(memory_space=pltpu.VMEM),
        scratch_shapes=[
            pltpu.VMEM((2048, 1024), BF16),
            pltpu.VMEM((6, 2, 2, 256, 128), F32), pltpu.VMEM((6, 2, 256, 128), F32), pltpu.VMEM((6, 4, 128, 128), F32),
            pltpu.VMEM((6, 3, 128, 128), F32), pltpu.VMEM((6, 4, 4, 8, 128), F32), pltpu.VMEM((6, 15, 8, 128), F32),
            dma((4,)), dma((6,)), dma((6,)), dma((6, 3)), dma((6, 3)), dma((6, 15)), dma((6, 15)),
            dma((6, 15)), dma((6, 15)), dma((6, 3)), dma((6, 3)), dma((6, 4)), dma((6, 4)),
        ],
        compiler_params=pltpu.CompilerParams(vmem_limit_bytes=56 * 1024 * 1024, collective_id=0, has_side_effects=True),
        name="gram_sum",
    )(x, pdev, prow)


def inverse_factors(augs, panels, first, work=()):
    sub = lax.broadcasted_iota(jnp.int32, (8, 128), 0)
    spread = lambda v, c: jnp.broadcast_to(v[:, c:c + 1], (8, 128))
    one = lambda v, r: jnp.broadcast_to(v[r:r + 1, :], (8, 128))
    every = range(len(augs))
    work, done = list(work), 0
    groups = [[aug[8 * q:8 * q + 8, :] for q in range(panels)] for aug in augs]
    outs = [[] for _ in every]
    late = []

    def columns_of(n, q, p):
        return [spread(groups[n][q], first + 8 * p + c) for c in range(8)]

    def reduce(n, q, columns, lines):
        terms = [columns[r] * lines[r] for r in range(8)]
        while len(terms) > 1:
            terms = [terms[i] + terms[i + 1] for i in range(0, len(terms), 2)]
        groups[n][q] = groups[n][q] - terms[0]

    for p in range(panels):
        v = [groups[n][p] for n in every]
        out = list(v)
        columns = [columns_of(n, p, p) for n in every]
        below = {}
        for r in range(8):
            for n in every:
                here = columns[n][r]
                pivot = one(here, r)
                inverse = 1.0 / pivot
                line = one(v[n], r)
                for c in range(r + 1, 8):
                    value = one(columns[n][c], r) * inverse
                    columns[n][c] = jnp.where(sub == r, value, columns[n][c] - here * value)
                out[n] = jnp.where(sub == r, line * lax.rsqrt(pivot), out[n])
                line = line * inverse
                v[n] = jnp.where(sub == r, line, v[n] - here * line)
            share = -(-len(late) // max(1, 6 - r))
            for n, q, lines in late[:share]:
                reduce(n, q, columns_of(n, q, p - 1), lines)
            late = late[share:]
            if r == 5 and p + 1 < panels:
                assert not late
                below = {n: columns_of(n, p + 1, p) for n in every}
            target = len(work) * (8 * p + r + 1) // (8 * panels)
            while done < target:
                work[done]()
                done += 1
        for n in every:
            outs[n].append(out[n])
            lines = [one(v[n], r) for r in range(8)]
            if p + 1 < panels:
                reduce(n, p + 1, below[n], lines)
            late += [(n, q, lines) for q in range(p + 2, panels)]
        late.sort(key=lambda item: item[1])
    return [jnp.concatenate(o, axis=0) for o in outs]


def iterate_kernel(inv_rows, b_ref, start_ref, x_hbm, modes_hbm, scores_ref, pb_ref,
                   gh, gl, sh, sl, yh, yl, qh, ql, th, tl, wh, wl, zh, zl, zf, x_ref, modes_ref, basis_ref,
                   x_sem, modes_sem):
    load = pltpu.make_async_copy(x_hbm, x_ref, x_sem)
    load.start()
    for n, (i, j) in enumerate(PAIRS):
        block = jnp.concatenate([b_ref[n % 2, n // 2, 0], b_ref[n % 2, n // 2, 1]], axis=1)
        hi, lo = split(block)
        gh[pl.ds(256 * i, 256), pl.ds(256 * j, 256)] = hi
        gl[pl.ds(256 * i, 256), pl.ds(256 * j, 256)] = lo
        if i != j:
            hi, lo = split(block.T)
            gh[pl.ds(256 * j, 256), pl.ds(256 * i, 256)] = hi
            gl[pl.ds(256 * j, 256), pl.ds(256 * i, 256)] = lo
    sh[...], sl[...] = split(start_ref[...].T)

    def times_gram(hi, lo):
        return dot(hi, gh[...], NN) + (dot(hi, gl[...], NN) + dot(lo, gh[...], NN))

    def block(j):
        return pl.ds(NB * j, NB)

    yh[0, block(0), :], yl[0, block(0), :] = split(times_gram(sh[block(0), :], sl[block(0), :]))
    th[...] = jnp.zeros_like(th)
    tl[...] = jnp.zeros_like(tl)

    row = lax.broadcasted_iota(jnp.int32, (NB, 256), 0)
    lane = lax.broadcasted_iota(jnp.int32, (NB, 256), 1)
    eye = (row == lane)[:, :NB].astype(F32)

    def stacked3(a, b, dims):
        n = a[0].shape[0]
        both = dot(jnp.concatenate([a[0], a[1]], axis=0), b[0], dims)
        return both[:n] + both[n:] + dot(a[0], b[1], dims)

    for t in range(8):
        tasks = [(t - j, j) for j in range(NJ) if 0 <= t - j <= 4]
        go = [(k, j) for k, j in tasks if k < 4]
        ahead = t < 3
        ms, ds, lows, vaug, coefs, part = {}, {}, {}, {}, {}, {}

        def left(k, where, lanes=slice(None)):
            return (yh[k, where, lanes], yl[k, where, lanes]) if k < 4 else (qh[where, lanes], ql[where, lanes])

        for k, j in tasks:
            scale = inv_rows if k == 4 else 1.0
            a = left(k, block(j))
            ds[k] = stacked3(a, (yh[k, block(j), :], yl[k, block(j), :]), NT) * scale
            if j > 0:
                before = pl.ds(0, NB * j)
                ms[k] = split(stacked3(a, (yh[k, before, :], yl[k, before, :]), NT) * scale)
        for k, j in tasks:
            if j > 0:
                before = pl.ds(0, NB * j)
                lows[k] = split(stacked3(ms[k], (th[k, before, before], tl[k, before, before]), NT))
        for k, j in tasks:
            if j > 0:
                ds[k] = ds[k] - stacked3(lows[k], lows[k], NT)

        def make_v(k, j):
            v = (lane == row + NB * j).astype(F32)
            if j > 0:
                coef = stacked3(lows[k], (th[k, pl.ds(0, NB * j), :], tl[k, pl.ds(0, NB * j), :]), NN)
                v = v - coef
                coefs[k] = split(coef[:, :NB * j])
            vaug[k] = split(v)

        def make_w(n, k, j, lanes):
            a = left(k, block(j), lanes)
            if j > 0:
                w = a[0].astype(F32) + a[1].astype(F32)
                a = split(w - stacked3(coefs[k], left(k, pl.ds(0, NB * j), lanes), NN))
            wh[block(n), lanes], wl[block(n), lanes] = a

        def make_ahead():
            n = len(go)
            wh[block(n), :], wl[block(n), :] = sh[block(t + 1), :], sl[block(t + 1), :]

        rows = NB * (len(go) + ahead)

        def make_z(lanes, depth, last):
            new = stacked3((wh[:rows, depth], wl[:rows, depth]), (gh[depth, lanes], gl[depth, lanes]), NN)
            part[0] = new if depth.start == 0 else part[0] + new
            if last:
                zh[:rows, lanes], zl[:rows, lanes] = split(part[0])

        work = [functools.partial(make_v, k, j) for k, j in tasks]
        work += [functools.partial(make_w, n, k, j, slice(512 * i, 512 * i + 512))
                 for n, (k, j) in enumerate(go + [task for task in tasks if task not in go]) for i in range(2)]
        if ahead:
            work.append(make_ahead)
        if rows:
            work += [functools.partial(make_z, slice(256 * i, 256 * i + 256), slice(256 * d, 256 * d + 256), d == 3)
                     for i in range(4) for d in range(4)]
        invs = inverse_factors([jnp.concatenate([eye, ds[k]], axis=1) for k, j in tasks], 8, NB, work)
        invs = {k: split(inv[:, :NB]) for (k, j), inv in zip(tasks, invs)}
        for n, (k, j) in enumerate(go):
            yh[k + 1, block(j), :], yl[k + 1, block(j), :] = split(stacked3(invs[k], (zh[block(n), :], zl[block(n), :]), NN))
            if k == 3:
                qh[block(j), :], ql[block(j), :] = split(stacked3(invs[k], (wh[block(n), :], wl[block(n), :]), NN))
        if ahead:
            n = len(go)
            yh[0, block(t + 1), :], yl[0, block(t + 1), :] = zh[block(n), :], zl[block(n), :]
        for k, j in tasks:
            if j < NJ - 1:
                th[k, block(j), :], tl[k, block(j), :] = split(stacked3(invs[k], vaug[k], NN))
            if k == 4:
                n = len(go)
                zf[block(j), :] = stacked3(invs[k], (wh[block(n), :], wl[block(n), :]), NN).astype(BF16)

    coef = zf[...]
    for part in range(4):
        here = pl.ds(32 * part, 32)
        xs = jnp.concatenate([b_ref[0, 5, 0, here, :], b_ref[0, 5, 1, here, :]], axis=1).astype(BF16)
        term = dot(xs, coef[:, 256 * part:256 * (part + 1)], NT)
        panel = term if part == 0 else panel + term
    ph = split(panel)
    small = jnp.concatenate(
        [eye[:32, :32], dot3(ph, ph, NT), jnp.zeros((32, 64), F32)], axis=1)

    load.wait()
    stores = []
    for n in range(8):
        here = pl.ds(256 * n, 256)
        basis = dot(x_ref[here, :], coef, NT)
        basis_ref[here, :] = basis
        modes_ref[here, :] = basis.astype(BF16)
        stores.append(pltpu.make_async_copy(modes_ref.at[here, :], modes_hbm.at[here, :], modes_sem.at[n]))
        stores[-1].start()

    inv = split(inverse_factors([small], 4, 32)[0][:, :32])
    pbt = dot3(inv, ph, NN)
    pb_ref[...] = pbt
    pb = split(pbt.T)
    proj = split(dot3(pb, pb, NT))
    ones = jnp.ones((8, 256), BF16)
    for n in range(8):
        here = pl.ds(256 * n, 256)
        basis = basis_ref[here, :]
        remaining = basis - dot3(split(basis), proj, NN)
        hi, lo = split(remaining * remaining)
        total = dot(ones, hi, NT) + dot(ones, lo, NT)
        scores_ref[2 * n:2 * n + 1, :] = total[:1, :128] * (1.0 / 256)
        scores_ref[2 * n + 1:2 * n + 2, :] = total[:1, 128:] * (1.0 / 256)
    for copy in stores:
        copy.wait()


def iterate_call(packed, start, x, inv_rows):
    vmem = lambda: pl.BlockSpec(memory_space=pltpu.VMEM)
    hbm = lambda: pl.BlockSpec(memory_space=pltpu.HBM)
    rows = x.shape[0]
    return pl.pallas_call(
        functools.partial(iterate_kernel, inv_rows),
        out_shape=(jax.ShapeDtypeStruct((rows, 256), BF16), jax.ShapeDtypeStruct((rows // 128, 128), F32),
                   jax.ShapeDtypeStruct((32, 256), F32)),
        in_specs=[vmem(), vmem(), hbm()],
        out_specs=(hbm(), vmem(), vmem()),
        scratch_shapes=[
            pltpu.VMEM((1024, 1024), BF16), pltpu.VMEM((1024, 1024), BF16),
            pltpu.VMEM((256, 1024), BF16), pltpu.VMEM((256, 1024), BF16),
            pltpu.VMEM((5, 256, 1024), BF16), pltpu.VMEM((5, 256, 1024), BF16),
            pltpu.VMEM((256, 1024), BF16), pltpu.VMEM((256, 1024), BF16),
            pltpu.VMEM((5, 256, 256), BF16), pltpu.VMEM((5, 256, 256), BF16),
            pltpu.VMEM((256, 1024), BF16), pltpu.VMEM((256, 1024), BF16),
            pltpu.VMEM((256, 1024), BF16), pltpu.VMEM((256, 1024), BF16),
            pltpu.VMEM((256, 1024), BF16),
            pltpu.VMEM((rows, 1024), BF16), pltpu.VMEM((rows, 256), BF16), pltpu.VMEM((rows, 256), F32),
            pltpu.SemaphoreType.DMA, pltpu.SemaphoreType.DMA((8,)),
        ],
        compiler_params=pltpu.CompilerParams(vmem_limit_bytes=50 * 1024 * 1024),
        name="iterate",
    )(packed, start, x)


def local(snapshots, start, pivot_dev, pivot_row):
    rows_total = snapshots.shape[0] * lax.axis_size(AXES)
    packed = reduce_call(snapshots, pivot_dev, pivot_row)
    modes, scores, panel_basis = iterate_call(packed.reshape(2, 6, 2, 256, 128), start, snapshots, 1.0 / rows_total)
    return (modes, scores.reshape(-1), panel_basis.T)


def solution(mesh):
    torus = Mesh(mesh.devices.reshape(4, 4, 4, 2), AXES)
    rows = ("y", "core", "x", "z")
    return jax.shard_map(
        local,
        mesh=torus,
        in_specs=(P(rows, None), P(), P(), P()),
        out_specs=(P(rows, None), P(rows), P()),
        check_vma=False,
    )
```

```python
import functools
import jax, jax.numpy as jnp
from jax import lax
from jax.experimental import pallas as pl
from jax.experimental.pallas import tpu as pltpu
from jax.sharding import Mesh
from jax.sharding import PartitionSpec as P

MESH = pl.DeviceIdType.MESH
F32, BF16 = jnp.float32, jnp.bfloat16
NB = 64
NJ = 4
PAIRS = [(0, 0), (0, 1), (0, 2), (0, 3), (1, 1), (1, 2), (1, 3), (2, 2), (2, 3), (3, 3)]

NN = (((1,), (0,)), ((), ()))
NT = (((1,), (1,)), ((), ()))


def split(x):
    hi = x.astype(BF16)
    return hi, (x - hi.astype(F32)).astype(BF16)


def dot(a, b, dims):
    return lax.dot_general(a, b, dims, preferred_element_type=F32)


def dot3(a, b, dims):
    return dot(a[0], b[0], dims) + (dot(a[0], b[1], dims) + dot(a[1], b[0], dims))


AXES = ("x", "z", "y", "core")
TURNS = (("x", "y", "z"), ("y", "z", "x"), ("z", "x", "y"))


def reduce_kernel(x_hbm, start_hbm, pdev_ref, prow_ref, gh_ref, gl_ref, sh_ref, sl_ref, xp_ref, full, x_ref, start_ref, loc, r0, acc, r1, a1, r2, x_sem, start_sem,
                  send0, recv0, send1, recv1, send2, recv2, send3, recv3, send4, recv4, send5, recv5):
    at = {name: lax.axis_index(name) for name in AXES}
    core = at["core"]
    other = 1 - core

    slabs = [pltpu.make_async_copy(x_hbm.at[:, pl.ds(256 * i, 256)], x_ref.at[:, pl.ds(256 * i, 256)], x_sem.at[i])
             for i in range(4)]
    for slab in slabs:
        slab.start()
    fetch = pltpu.make_async_copy(start_hbm, start_ref, start_sem)
    fetch.start()

    def axis_peers(axis):
        return [(d - 1, {axis: lax.rem(at[axis] + d, 4)}) for d in (1, 2, 3)]

    def plane_peers(m):
        one, two = TURNS[m % 3][1:]
        return [(4 * d + e - 1, {one: lax.rem(at[one] + d, 4), two: lax.rem(at[two] + e, 4)})
                for d in range(4) for e in range(4) if d or e]

    barrier = pltpu.get_barrier_semaphore()
    pl.semaphore_signal(barrier, inc=1, device_id={"core": other}, device_id_type=MESH)
    for axis in ("x", "y", "z"):
        for _, peer in axis_peers(axis):
            pl.semaphore_signal(barrier, inc=1, device_id=peer, device_id_type=MESH)
    for c in range(3):
        for slot, peer in plane_peers(c):
            if (slot + 1) // 4 and (slot + 1) % 4:
                pl.semaphore_signal(barrier, inc=1, device_id=peer, device_id_type=MESH)

    sent = []

    def go(src, dst, send, recv, peer):
        copy = pltpu.make_async_remote_copy(src_ref=src, dst_ref=dst, send_sem=send, recv_sem=recv,
                                            device_id=peer, device_id_type=MESH)
        copy.start()
        sent.append(copy)
        return copy

    def keep(m, half, value):
        loc[m, half, 0] = value[:, :128]
        loc[m, half, 1] = value[:, 128:]

    def pair(m):
        for half in (0, 1):
            n = 2 * m + half
            if n < 10:
                i, j = PAIRS[n]
                keep(m, half, lax.dot_general(x_ref[:, 256 * i:256 * i + 256], x_ref[:, 256 * j:256 * j + 256],
                                              (((0,), (0,)), ((), ())), preferred_element_type=F32))
            elif n == 10:
                me = ((at["y"] * 2 + core) * 4 + at["x"]) * 4 + at["z"]
                pivot = lax.broadcasted_iota(jnp.int32, (32, 128), 0)
                lane = lax.broadcasted_iota(jnp.int32, (32, 128), 1)
                target = jnp.full((32, 128), -1, jnp.int32)
                for i in range(32):
                    target = jnp.where(pivot == i, jnp.where(pdev_ref[i] == me, prow_ref[i], -1), target)
                hit = jnp.concatenate([(target == lane + 128 * i).astype(F32).astype(BF16) for i in range(16)], axis=1)
                picked = dot(hit, x_ref[...], NN)
                keep(m, half, jnp.concatenate([picked[:, 256 * part:256 * part + 256] for part in range(4)]
                                              + [jnp.zeros((128, 256), F32)], axis=0))
            else:
                keep(m, half, jnp.zeros((256, 256), F32))

    swaps, down, across, back, up, over = {}, {}, {}, {}, {}, {}

    def swap(m):
        swaps[m] = go(loc.at[m, other], r0.at[m], send0.at[m], recv0.at[m], {"core": other})

    def down1(m):
        swaps[m].wait_recv()
        for i in range(2):
            total = loc[m, core, i] + r0[m, i]
            acc[m, 2 * i] = total[:128]
            acc[m, 2 * i + 1] = total[128:]
        axis = TURNS[m % 3][0]
        down[m] = [go(acc.at[m, peer[axis]], r1.at[m, slot], send1.at[m, slot], recv1.at[m, slot], peer)
                   for slot, peer in axis_peers(axis)]

    def down2(m):
        for copy in down[m]:
            copy.wait_recv()
        total = (acc[m, at[TURNS[m % 3][0]]] + r1[m, 0]) + (r1[m, 1] + r1[m, 2])
        for i in range(16):
            a1[m, i // 4, i % 4] = total[8 * i:8 * i + 8]
        one, two = TURNS[m % 3][1:]
        across[m] = [go(a1.at[m, peer[one], peer[two]], r2.at[m, slot], send2.at[m, slot], recv2.at[m, slot], peer)
                     for slot, peer in plane_peers(m)]

    def up2(m):
        for copy in across[m]:
            copy.wait_recv()
        one, two, three = (at[name] for name in TURNS[m % 3])
        terms = [a1[m, two, three]] + [r2[m, slot] for slot in range(15)]
        while len(terms) > 1:
            terms = [terms[i] + terms[i + 1] for i in range(0, len(terms), 2)]
        rows = pl.ds(pl.multiple_of(8 * (16 * one + 4 * two + three), 8), 8)
        full[core, m, rows, :] = terms[0]
        mine = full.at[core, m, rows, :]
        back[m] = [go(mine, mine, send3.at[m, slot], recv3.at[m, slot], peer) for slot, peer in plane_peers(m)]

    def up1(m):
        for copy in back[m]:
            copy.wait_recv()
        axis = TURNS[m % 3][0]
        mine = full.at[core, m, pl.ds(pl.multiple_of(128 * at[axis], 128), 128), :]
        up[m] = [go(mine, mine, send4.at[m, slot], recv4.at[m, slot], peer) for slot, peer in axis_peers(axis)]
        over[m] = [go(mine, mine, send5.at[m, 3], recv5.at[m, 3], {"core": other})]

    def forward(m, slot):
        up[m][slot].wait_recv()
        piece = full.at[core, m, pl.ds(pl.multiple_of(128 * lax.rem(at[TURNS[m % 3][0]] + 3 - slot, 4), 128), 128), :]
        over[m].append(go(piece, piece, send5.at[m, slot], recv5.at[m, slot], {"core": other}))

    same = lax.broadcasted_iota(jnp.int32, (256, 256), 0) == lax.broadcasted_iota(jnp.int32, (256, 256), 1)
    eye = same.astype(F32).astype(BF16)

    def turn(v):
        return lax.dot_general(v, eye, (((0,), (0,)), ((), ())), preferred_element_type=F32).astype(BF16)

    def give(m):
        for copy in over[m]:
            copy.wait_recv()
        for half in (0, 1):
            n = 2 * m + half
            if n < 10:
                i, j = PAIRS[n]
                upper = pl.ds(256 * i, 256), pl.ds(256 * j, 256)
                lower = pl.ds(256 * j, 256), pl.ds(256 * i, 256)
                hi, lo = split(jnp.concatenate([full[half, m, 0:256, :], full[half, m, 256:512, :]], axis=1))
                gh_ref[upper], gl_ref[upper] = hi, lo
                if i != j:
                    gh_ref[lower], gl_ref[lower] = turn(hi), turn(lo)
            elif n == 10:
                for part in range(4):
                    for i in range(2):
                        value = full[half, m, 256 * i + 32 * part:256 * i + 32 * part + 32, :]
                        xp_ref[:, 256 * part + 128 * i:256 * part + 128 * i + 128] = value.astype(BF16)

    def turn_start():
        fetch.wait()
        for part in range(4):
            here = pl.ds(256 * part, 256)
            hi, lo = split(start_ref[here, :])
            sh_ref[:, here], sl_ref[:, here] = turn(hi), turn(lo)

    early, late = (0, 1, 2), (3, 4, 5)
    for m in early:
        for slab in slabs[2 * m:2 * m + 2]:
            slab.wait()
        pair(m)
    pl.semaphore_wait(barrier, 37)
    for m in early:
        swap(m)
    pair(3)
    swap(3)
    for m in early:
        down1(m)
    pair(4)
    swap(4)
    pair(5)
    swap(5)
    for m in late:
        down1(m)
    turn_start()
    for stage, units in ((down2, early), (down2, late), (up2, early), (up2, late), (up1, early), (up1, late)):
        for m in units:
            stage(m)
    for units in (early, late):
        for slot in (0, 2, 1):
            for m in units:
                forward(m, slot)
        for m in units:
            give(m)
    for copy in sent:
        copy.wait_send()


def reduce_call(x, start, pdev, prow):
    dma = pltpu.SemaphoreType.DMA
    return pl.pallas_call(
        reduce_kernel,
        out_shape=tuple(jax.ShapeDtypeStruct(shape, BF16)
                        for shape in ((1024, 1024), (1024, 1024), (256, 1024), (256, 1024), (32, 1024))),
        in_specs=[pl.BlockSpec(memory_space=pltpu.HBM)] * 2 + [pl.BlockSpec(memory_space=pltpu.SMEM)] * 2,
        out_specs=(pl.BlockSpec(memory_space=pltpu.VMEM),) * 5,
        scratch_shapes=[
            pltpu.VMEM((2, 6, 512, 128), F32), pltpu.VMEM((2048, 1024), BF16), pltpu.VMEM((1024, 256), F32),
            pltpu.VMEM((6, 2, 2, 256, 128), F32), pltpu.VMEM((6, 2, 256, 128), F32), pltpu.VMEM((6, 4, 128, 128), F32),
            pltpu.VMEM((6, 3, 128, 128), F32), pltpu.VMEM((6, 4, 4, 8, 128), F32), pltpu.VMEM((6, 15, 8, 128), F32),
            dma((4,)), dma(()), dma((6,)), dma((6,)), dma((6, 3)), dma((6, 3)), dma((6, 15)), dma((6, 15)),
            dma((6, 15)), dma((6, 15)), dma((6, 3)), dma((6, 3)), dma((6, 4)), dma((6, 4)),
        ],
        compiler_params=pltpu.CompilerParams(vmem_limit_bytes=56 * 1024 * 1024, collective_id=0, has_side_effects=True),
        name="gram_sum",
    )(x, start, pdev, prow)


def inverse_factors(augs, panels, first, work=()):
    sub = lax.broadcasted_iota(jnp.int32, (8, 128), 0)
    spread = lambda v, c: jnp.broadcast_to(v[:, c:c + 1], (8, 128))
    one = lambda v, r: jnp.broadcast_to(v[r:r + 1, :], (8, 128))
    every = range(len(augs))
    work, done = list(work), 0
    groups = [[aug[8 * q:8 * q + 8, :] for q in range(panels)] for aug in augs]
    outs = [[] for _ in every]
    late = []

    def columns_of(n, q, p):
        return [spread(groups[n][q], first + 8 * p + c) for c in range(8)]

    def reduce(n, q, columns, lines):
        terms = [columns[r] * lines[r] for r in range(8)]
        while len(terms) > 1:
            terms = [terms[i] + terms[i + 1] for i in range(0, len(terms), 2)]
        groups[n][q] = groups[n][q] - terms[0]

    for p in range(panels):
        v = [groups[n][p] for n in every]
        out = list(v)
        columns = [columns_of(n, p, p) for n in every]
        below = {}
        for r in range(8):
            for n in every:
                here = columns[n][r]
                pivot = one(here, r)
                inverse = 1.0 / pivot
                line = one(v[n], r)
                for c in range(r + 1, 8):
                    value = one(columns[n][c], r) * inverse
                    columns[n][c] = jnp.where(sub == r, value, columns[n][c] - here * value)
                out[n] = jnp.where(sub == r, line * lax.rsqrt(pivot), out[n])
                line = line * inverse
                v[n] = jnp.where(sub == r, line, v[n] - here * line)
            share = -(-len(late) // max(1, 6 - r))
            for n, q, lines in late[:share]:
                reduce(n, q, columns_of(n, q, p - 1), lines)
            late = late[share:]
            if r == 5 and p + 1 < panels:
                assert not late
                below = {n: columns_of(n, p + 1, p) for n in every}
            target = len(work) * (8 * p + r + 1) // (8 * panels)
            while done < target:
                work[done]()
                done += 1
        for n in every:
            outs[n].append(out[n])
            lines = [one(v[n], r) for r in range(8)]
            if p + 1 < panels:
                reduce(n, p + 1, below[n], lines)
            late += [(n, q, lines) for q in range(p + 2, panels)]
        late.sort(key=lambda item: item[1])
    return [jnp.concatenate(o, axis=0) for o in outs]


def iterate_kernel(inv_rows, gh, gl, sh, sl, xp_ref, x_hbm, modes_hbm, scores_ref, pb_ref,
                   yh, yl, qh, ql, th, tl, wh, wl, zh, zl, zf, x_ref, modes_ref, basis_ref,
                   x_sem, modes_sem):
    load = pltpu.make_async_copy(x_hbm, x_ref, x_sem)
    load.start()
    def times_gram(hi, lo):
        return dot(hi, gh[...], NN) + (dot(hi, gl[...], NN) + dot(lo, gh[...], NN))

    def block(j):
        return pl.ds(NB * j, NB)

    yh[0, block(0), :], yl[0, block(0), :] = split(times_gram(sh[block(0), :], sl[block(0), :]))
    th[...] = jnp.zeros_like(th)
    tl[...] = jnp.zeros_like(tl)

    row = lax.broadcasted_iota(jnp.int32, (NB, 256), 0)
    lane = lax.broadcasted_iota(jnp.int32, (NB, 256), 1)
    eye = (row == lane)[:, :NB].astype(F32)

    def stacked3(a, b, dims):
        n = a[0].shape[0]
        both = dot(jnp.concatenate([a[0], a[1]], axis=0), b[0], dims)
        return both[:n] + both[n:] + dot(a[0], b[1], dims)

    for t in range(8):
        tasks = [(t - j, j) for j in range(NJ) if 0 <= t - j <= 4]
        go = [(k, j) for k, j in tasks if k < 4]
        ahead = t < 3
        ms, ds, lows, vaug, coefs, part = {}, {}, {}, {}, {}, {}

        def left(k, where, lanes=slice(None)):
            return (yh[k, where, lanes], yl[k, where, lanes]) if k < 4 else (qh[where, lanes], ql[where, lanes])

        for k, j in tasks:
            scale = inv_rows if k == 4 else 1.0
            a = left(k, block(j))
            ds[k] = stacked3(a, (yh[k, block(j), :], yl[k, block(j), :]), NT) * scale
            if j > 0:
                before = pl.ds(0, NB * j)
                ms[k] = split(stacked3(a, (yh[k, before, :], yl[k, before, :]), NT) * scale)
        for k, j in tasks:
            if j > 0:
                before = pl.ds(0, NB * j)
                lows[k] = split(stacked3(ms[k], (th[k, before, before], tl[k, before, before]), NT))
        for k, j in tasks:
            if j > 0:
                ds[k] = ds[k] - stacked3(lows[k], lows[k], NT)

        def make_v(k, j):
            v = (lane == row + NB * j).astype(F32)
            if j > 0:
                coef = stacked3(lows[k], (th[k, pl.ds(0, NB * j), :], tl[k, pl.ds(0, NB * j), :]), NN)
                v = v - coef
                coefs[k] = split(coef[:, :NB * j])
            vaug[k] = split(v)

        def make_w(n, k, j, lanes):
            a = left(k, block(j), lanes)
            if j > 0:
                w = a[0].astype(F32) + a[1].astype(F32)
                a = split(w - stacked3(coefs[k], left(k, pl.ds(0, NB * j), lanes), NN))
            wh[block(n), lanes], wl[block(n), lanes] = a

        def make_ahead():
            n = len(go)
            wh[block(n), :], wl[block(n), :] = sh[block(t + 1), :], sl[block(t + 1), :]

        rows = NB * (len(go) + ahead)

        def make_z(lanes, depth, last):
            new = stacked3((wh[:rows, depth], wl[:rows, depth]), (gh[depth, lanes], gl[depth, lanes]), NN)
            part[0] = new if depth.start == 0 else part[0] + new
            if last:
                zh[:rows, lanes], zl[:rows, lanes] = split(part[0])

        work = [functools.partial(make_v, k, j) for k, j in tasks]
        work += [functools.partial(make_w, n, k, j, slice(512 * i, 512 * i + 512))
                 for n, (k, j) in enumerate(go + [task for task in tasks if task not in go]) for i in range(2)]
        if ahead:
            work.append(make_ahead)
        if rows:
            work += [functools.partial(make_z, slice(256 * i, 256 * i + 256), slice(256 * d, 256 * d + 256), d == 3)
                     for i in range(4) for d in range(4)]
        invs = inverse_factors([jnp.concatenate([eye, ds[k]], axis=1) for k, j in tasks], 8, NB, work)
        invs = {k: split(inv[:, :NB]) for (k, j), inv in zip(tasks, invs)}
        for n, (k, j) in enumerate(go):
            yh[k + 1, block(j), :], yl[k + 1, block(j), :] = split(stacked3(invs[k], (zh[block(n), :], zl[block(n), :]), NN))
            if k == 3:
                qh[block(j), :], ql[block(j), :] = split(stacked3(invs[k], (wh[block(n), :], wl[block(n), :]), NN))
        if ahead:
            n = len(go)
            yh[0, block(t + 1), :], yl[0, block(t + 1), :] = zh[block(n), :], zl[block(n), :]
        for k, j in tasks:
            if j < NJ - 1:
                th[k, block(j), :], tl[k, block(j), :] = split(stacked3(invs[k], vaug[k], NN))
            if k == 4:
                n = len(go)
                zf[block(j), :] = stacked3(invs[k], (wh[block(n), :], wl[block(n), :]), NN).astype(BF16)

    coef = zf[...]
    panel = dot(xp_ref[...], coef, NT)
    ph = split(panel)
    small = jnp.concatenate(
        [eye[:32, :32], dot3(ph, ph, NT), jnp.zeros((32, 64), F32)], axis=1)

    load.wait()
    stores = []

    def make_basis(n):
        here = pl.ds(256 * n, 256)
        basis = dot(x_ref[here, :], coef, NT)
        basis_ref[here, :] = basis
        modes_ref[here, :] = basis.astype(BF16)
        stores.append(pltpu.make_async_copy(modes_ref.at[here, :], modes_hbm.at[here, :], modes_sem.at[n]))
        stores[-1].start()

    inv = split(inverse_factors([small], 4, 32, [functools.partial(make_basis, n) for n in range(8)])[0][:, :32])
    pbt = dot3(inv, ph, NN)
    pb_ref[...] = pbt
    pb = split(pbt.T)
    proj = split(dot3(pb, pb, NT))
    ones = jnp.ones((8, 256), BF16)
    for n in range(8):
        here = pl.ds(256 * n, 256)
        basis = basis_ref[here, :]
        remaining = basis - dot3(split(basis), proj, NN)
        hi, lo = split(remaining * remaining)
        total = dot(ones, hi, NT) + dot(ones, lo, NT)
        scores_ref[2 * n:2 * n + 1, :] = total[:1, :128] * (1.0 / 256)
        scores_ref[2 * n + 1:2 * n + 2, :] = total[:1, 128:] * (1.0 / 256)
    for copy in stores:
        copy.wait()


def iterate_call(gh, gl, sh, sl, xp, x, inv_rows):
    vmem = lambda: pl.BlockSpec(memory_space=pltpu.VMEM)
    hbm = lambda: pl.BlockSpec(memory_space=pltpu.HBM)
    rows = x.shape[0]
    return pl.pallas_call(
        functools.partial(iterate_kernel, inv_rows),
        out_shape=(jax.ShapeDtypeStruct((rows, 256), BF16), jax.ShapeDtypeStruct((rows // 128, 128), F32),
                   jax.ShapeDtypeStruct((32, 256), F32)),
        in_specs=[vmem(), vmem(), vmem(), vmem(), vmem(), hbm()],
        out_specs=(hbm(), vmem(), vmem()),
        scratch_shapes=[
            pltpu.VMEM((5, 256, 1024), BF16), pltpu.VMEM((5, 256, 1024), BF16),
            pltpu.VMEM((256, 1024), BF16), pltpu.VMEM((256, 1024), BF16),
            pltpu.VMEM((5, 256, 256), BF16), pltpu.VMEM((5, 256, 256), BF16),
            pltpu.VMEM((256, 1024), BF16), pltpu.VMEM((256, 1024), BF16),
            pltpu.VMEM((256, 1024), BF16), pltpu.VMEM((256, 1024), BF16),
            pltpu.VMEM((256, 1024), BF16),
            pltpu.VMEM((rows, 1024), BF16), pltpu.VMEM((rows, 256), BF16), pltpu.VMEM((rows, 256), F32),
            pltpu.SemaphoreType.DMA, pltpu.SemaphoreType.DMA((8,)),
        ],
        compiler_params=pltpu.CompilerParams(vmem_limit_bytes=56 * 1024 * 1024),
        name="iterate",
    )(gh, gl, sh, sl, xp, x)


def local(snapshots, start, pivot_dev, pivot_row):
    rows_total = snapshots.shape[0] * lax.axis_size(AXES)
    parts = reduce_call(snapshots, start, pivot_dev, pivot_row)
    modes, scores, panel_basis = iterate_call(*parts, snapshots, 1.0 / rows_total)
    return (modes, scores.reshape(-1), panel_basis.T)


def solution(mesh):
    torus = Mesh(mesh.devices.reshape(4, 4, 4, 2), AXES)
    rows = ("y", "core", "x", "z")
    return jax.shard_map(
        local,
        mesh=torus,
        in_specs=(P(rows, None), P(), P(), P()),
        out_specs=(P(rows, None), P(rows), P()),
        check_vma=False,
    )
```

```python
import functools
import jax, jax.numpy as jnp
from jax import lax
from jax.experimental import pallas as pl
from jax.experimental.pallas import tpu as pltpu
from jax.sharding import Mesh
from jax.sharding import PartitionSpec as P

MESH = pl.DeviceIdType.MESH
F32, BF16 = jnp.float32, jnp.bfloat16
NB = 64
NJ = 4
PAIRS = [(0, 0), (0, 1), (0, 2), (0, 3), (1, 1), (1, 2), (1, 3), (2, 2), (2, 3), (3, 3)]

NN = (((1,), (0,)), ((), ()))
NT = (((1,), (1,)), ((), ()))


def split(x):
    hi = x.astype(BF16)
    return hi, (x - hi.astype(F32)).astype(BF16)


def dot(a, b, dims):
    return lax.dot_general(a, b, dims, preferred_element_type=F32)


def dot3(a, b, dims):
    return dot(a[0], b[0], dims) + (dot(a[0], b[1], dims) + dot(a[1], b[0], dims))


AXES = ("x", "z", "y", "core")
TURNS = (("x", "y", "z"), ("y", "z", "x"), ("z", "x", "y"))


def reduce_kernel(x_hbm, pdev_ref, prow_ref, out_ref, x_ref, loc, r0, acc, r1, a1, r2, x_sem,
                  send0, recv0, send1, recv1, send2, recv2, send3, recv3, send4, recv4, send5, recv5):
    at = {name: lax.axis_index(name) for name in AXES}
    core = at["core"]
    other = 1 - core

    slabs = [pltpu.make_async_copy(x_hbm.at[:, pl.ds(256 * i, 256)], x_ref.at[:, pl.ds(256 * i, 256)], x_sem.at[i])
             for i in range(4)]
    for slab in slabs:
        slab.start()

    def axis_peers(axis):
        return [(d - 1, {axis: lax.rem(at[axis] + d, 4)}) for d in (1, 2, 3)]

    def plane_peers(m):
        one, two = TURNS[m % 3][1:]
        return [(4 * d + e - 1, {one: lax.rem(at[one] + d, 4), two: lax.rem(at[two] + e, 4)})
                for d in range(4) for e in range(4) if d or e]

    barrier = pltpu.get_barrier_semaphore()
    pl.semaphore_signal(barrier, inc=1, device_id={"core": other}, device_id_type=MESH)
    for axis in ("x", "y", "z"):
        for _, peer in axis_peers(axis):
            pl.semaphore_signal(barrier, inc=1, device_id=peer, device_id_type=MESH)
    for c in range(3):
        for slot, peer in plane_peers(c):
            if (slot + 1) // 4 and (slot + 1) % 4:
                pl.semaphore_signal(barrier, inc=1, device_id=peer, device_id_type=MESH)

    sent = []

    def go(src, dst, send, recv, peer):
        copy = pltpu.make_async_remote_copy(src_ref=src, dst_ref=dst, send_sem=send, recv_sem=recv,
                                            device_id=peer, device_id_type=MESH)
        copy.start()
        sent.append(copy)
        return copy

    def keep(m, half, value):
        loc[m, half, 0] = value[:, :128]
        loc[m, half, 1] = value[:, 128:]

    def pair(m):
        for half in (0, 1):
            n = 2 * m + half
            if n < 10:
                i, j = PAIRS[n]
                keep(m, half, lax.dot_general(x_ref[:, 256 * i:256 * i + 256], x_ref[:, 256 * j:256 * j + 256],
                                              (((0,), (0,)), ((), ())), preferred_element_type=F32))
            elif n == 10:
                me = ((at["y"] * 2 + core) * 4 + at["x"]) * 4 + at["z"]
                pivot = lax.broadcasted_iota(jnp.int32, (32, 128), 0)
                lane = lax.broadcasted_iota(jnp.int32, (32, 128), 1)
                target = jnp.full((32, 128), -1, jnp.int32)
                for i in range(32):
                    target = jnp.where(pivot == i, jnp.where(pdev_ref[i] == me, prow_ref[i], -1), target)
                hit = jnp.concatenate([(target == lane + 128 * i).astype(F32).astype(BF16) for i in range(16)], axis=1)
                picked = dot(hit, x_ref[...], NN)
                keep(m, half, jnp.concatenate([picked[:, 256 * part:256 * part + 256] for part in range(4)]
                                              + [jnp.zeros((128, 256), F32)], axis=0))
            else:
                keep(m, half, jnp.zeros((256, 256), F32))

    swaps, down, across, back, up, over = {}, {}, {}, {}, {}, []

    def swap(m):
        swaps[m] = go(loc.at[m, other], r0.at[m], send0.at[m], recv0.at[m], {"core": other})

    def down1(m):
        swaps[m].wait_recv()
        for i in range(2):
            total = loc[m, core, i] + r0[m, i]
            acc[m, 2 * i] = total[:128]
            acc[m, 2 * i + 1] = total[128:]
        axis = TURNS[m % 3][0]
        down[m] = [go(acc.at[m, peer[axis]], r1.at[m, slot], send1.at[m, slot], recv1.at[m, slot], peer)
                   for slot, peer in axis_peers(axis)]

    def down2(m):
        for copy in down[m]:
            copy.wait_recv()
        total = (acc[m, at[TURNS[m % 3][0]]] + r1[m, 0]) + (r1[m, 1] + r1[m, 2])
        for i in range(16):
            a1[m, i // 4, i % 4] = total[8 * i:8 * i + 8]
        one, two = TURNS[m % 3][1:]
        across[m] = [go(a1.at[m, peer[one], peer[two]], r2.at[m, slot], send2.at[m, slot], recv2.at[m, slot], peer)
                     for slot, peer in plane_peers(m)]

    def up2(m):
        for copy in across[m]:
            copy.wait_recv()
        one, two, three = (at[name] for name in TURNS[m % 3])
        terms = [a1[m, two, three]] + [r2[m, slot] for slot in range(15)]
        while len(terms) > 1:
            terms = [terms[i] + terms[i + 1] for i in range(0, len(terms), 2)]
        out_ref[core, m, one, two, three] = terms[0]
        mine = out_ref.at[core, m, one, two, three]
        back[m] = [go(mine, mine, send3.at[m, slot], recv3.at[m, slot], peer) for slot, peer in plane_peers(m)]

    def up1(m):
        for copy in back[m]:
            copy.wait_recv()
        axis = TURNS[m % 3][0]
        mine = out_ref.at[core, m, at[axis]]
        up[m] = [go(mine, mine, send4.at[m, slot], recv4.at[m, slot], peer) for slot, peer in axis_peers(axis)]
        over.append(go(mine, mine, send5.at[m, 3], recv5.at[m, 3], {"core": other}))

    def forward(m, slot):
        up[m][slot].wait_recv()
        piece = out_ref.at[core, m, lax.rem(at[TURNS[m % 3][0]] + 3 - slot, 4)]
        over.append(go(piece, piece, send5.at[m, slot], recv5.at[m, slot], {"core": other}))

    early, late = (0, 1, 2), (3, 4, 5)
    for m in early:
        for slab in slabs[2 * m:2 * m + 2]:
            slab.wait()
        pair(m)
    pl.semaphore_wait(barrier, 37)
    for m in early:
        swap(m)
    pair(3)
    swap(3)
    for m in early:
        down1(m)
    pair(4)
    swap(4)
    pair(5)
    swap(5)
    for stage, units in ((down1, late), (down2, early), (down2, late), (up2, early), (up2, late), (up1, early), (up1, late)):
        for m in units:
            stage(m)
    for units in (early, late):
        for slot in (0, 2, 1):
            for m in units:
                forward(m, slot)
    for copy in over:
        copy.wait_recv()
    for copy in sent:
        copy.wait_send()


def reduce_call(x, pdev, prow):
    dma = pltpu.SemaphoreType.DMA
    return pl.pallas_call(
        reduce_kernel,
        out_shape=jax.ShapeDtypeStruct((2, 6, 4, 4, 4, 8, 128), F32),
        in_specs=[pl.BlockSpec(memory_space=pltpu.HBM)] + [pl.BlockSpec(memory_space=pltpu.SMEM)] * 2,
        out_specs=pl.BlockSpec(memory_space=pltpu.VMEM),
        scratch_shapes=[
            pltpu.VMEM((2048, 1024), BF16),
            pltpu.VMEM((6, 2, 2, 256, 128), F32), pltpu.VMEM((6, 2, 256, 128), F32), pltpu.VMEM((6, 4, 128, 128), F32),
            pltpu.VMEM((6, 3, 128, 128), F32), pltpu.VMEM((6, 4, 4, 8, 128), F32), pltpu.VMEM((6, 15, 8, 128), F32),
            dma((4,)), dma((6,)), dma((6,)), dma((6, 3)), dma((6, 3)), dma((6, 15)), dma((6, 15)),
            dma((6, 15)), dma((6, 15)), dma((6, 3)), dma((6, 3)), dma((6, 4)), dma((6, 4)),
        ],
        compiler_params=pltpu.CompilerParams(vmem_limit_bytes=56 * 1024 * 1024, collective_id=0, has_side_effects=True),
        name="gram_sum",
    )(x, pdev, prow)


def inverse_factors(augs, panels, first, work=()):
    sub = lax.broadcasted_iota(jnp.int32, (8, 128), 0)
    spread = lambda v, c: jnp.broadcast_to(v[:, c:c + 1], (8, 128))
    one = lambda v, r: jnp.broadcast_to(v[r:r + 1, :], (8, 128))
    every = range(len(augs))
    work, done = list(work), 0
    groups = [[aug[8 * q:8 * q + 8, :] for q in range(panels)] for aug in augs]
    outs = [[] for _ in every]
    late = []

    def columns_of(n, q, p):
        return [spread(groups[n][q], first + 8 * p + c) for c in range(8)]

    def reduce(n, q, columns, lines):
        terms = [columns[r] * lines[r] for r in range(8)]
        while len(terms) > 1:
            terms = [terms[i] + terms[i + 1] for i in range(0, len(terms), 2)]
        groups[n][q] = groups[n][q] - terms[0]

    for p in range(panels):
        v = [groups[n][p] for n in every]
        out = list(v)
        columns = [columns_of(n, p, p) for n in every]
        below = {}
        for r in range(8):
            for n in every:
                here = columns[n][r]
                pivot = one(here, r)
                inverse = 1.0 / pivot
                line = one(v[n], r)
                for c in range(r + 1, 8):
                    value = one(columns[n][c], r) * inverse
                    columns[n][c] = jnp.where(sub == r, value, columns[n][c] - here * value)
                out[n] = jnp.where(sub == r, line * lax.rsqrt(pivot), out[n])
                line = line * inverse
                v[n] = jnp.where(sub == r, line, v[n] - here * line)
            share = -(-len(late) // max(1, 6 - r))
            for n, q, lines in late[:share]:
                reduce(n, q, columns_of(n, q, p - 1), lines)
            late = late[share:]
            if r == 5 and p + 1 < panels:
                assert not late
                below = {n: columns_of(n, p + 1, p) for n in every}
            target = len(work) * (8 * p + r + 1) // (8 * panels)
            while done < target:
                work[done]()
                done += 1
        for n in every:
            outs[n].append(out[n])
            lines = [one(v[n], r) for r in range(8)]
            if p + 1 < panels:
                reduce(n, p + 1, below[n], lines)
            late += [(n, q, lines) for q in range(p + 2, panels)]
        late.sort(key=lambda item: item[1])
    return [jnp.concatenate(o, axis=0) for o in outs]


def iterate_kernel(inv_rows, b_ref, start_ref, x_hbm, modes_hbm, scores_ref, pb_ref,
                   gh, gl, sh, sl, yh, yl, qh, ql, th, tl, wh, wl, zh, zl, zf, x_ref, modes_ref, basis_ref,
                   x_sem, modes_sem):
    load = pltpu.make_async_copy(x_hbm, x_ref, x_sem)
    load.start()
    for n, (i, j) in enumerate(PAIRS):
        block = jnp.concatenate([b_ref[n % 2, n // 2, 0], b_ref[n % 2, n // 2, 1]], axis=1)
        hi, lo = split(block)
        gh[pl.ds(256 * i, 256), pl.ds(256 * j, 256)] = hi
        gl[pl.ds(256 * i, 256), pl.ds(256 * j, 256)] = lo
        if i != j:
            hi, lo = split(block.T)
            gh[pl.ds(256 * j, 256), pl.ds(256 * i, 256)] = hi
            gl[pl.ds(256 * j, 256), pl.ds(256 * i, 256)] = lo
    sh[...], sl[...] = split(start_ref[...].T)

    def times_gram(hi, lo):
        return dot(hi, gh[...], NN) + (dot(hi, gl[...], NN) + dot(lo, gh[...], NN))

    def block(j):
        return pl.ds(NB * j, NB)

    yh[0, block(0), :], yl[0, block(0), :] = split(times_gram(sh[block(0), :], sl[block(0), :]))
    th[...] = jnp.zeros_like(th)
    tl[...] = jnp.zeros_like(tl)

    row = lax.broadcasted_iota(jnp.int32, (NB, 256), 0)
    lane = lax.broadcasted_iota(jnp.int32, (NB, 256), 1)
    eye = (row == lane)[:, :NB].astype(F32)

    def stacked3(a, b, dims):
        n = a[0].shape[0]
        both = dot(jnp.concatenate([a[0], a[1]], axis=0), b[0], dims)
        return both[:n] + both[n:] + dot(a[0], b[1], dims)

    for t in range(8):
        tasks = [(t - j, j) for j in range(NJ) if 0 <= t - j <= 4]
        go = [(k, j) for k, j in tasks if k < 4]
        ahead = t < 3
        ms, ds, lows, vaug, coefs, part = {}, {}, {}, {}, {}, {}

        def left(k, where, lanes=slice(None)):
            return (yh[k, where, lanes], yl[k, where, lanes]) if k < 4 else (qh[where, lanes], ql[where, lanes])

        for k, j in tasks:
            scale = inv_rows if k == 4 else 1.0
            a = left(k, block(j))
            upto = pl.ds(0, NB * (j + 1))
            both = stacked3(a, (yh[k, upto, :], yl[k, upto, :]), NT) * scale
            ds[k] = both[:, NB * j:]
            if j > 0:
                ms[k] = split(both[:, :NB * j])
        for k, j in tasks:
            if j > 0:
                before = pl.ds(0, NB * j)
                lows[k] = split(stacked3(ms[k], (th[k, before, before], tl[k, before, before]), NT))
        for k, j in tasks:
            if j > 0:
                ds[k] = ds[k] - stacked3(lows[k], lows[k], NT)

        def make_v(k, j):
            v = (lane == row + NB * j).astype(F32)
            if j > 0:
                coef = stacked3(lows[k], (th[k, pl.ds(0, NB * j), :], tl[k, pl.ds(0, NB * j), :]), NN)
                v = v - coef
                coefs[k] = split(coef[:, :NB * j])
            vaug[k] = split(v)

        def make_w(n, k, j, lanes):
            a = left(k, block(j), lanes)
            if j > 0:
                w = a[0].astype(F32) + a[1].astype(F32)
                a = split(w - stacked3(coefs[k], left(k, pl.ds(0, NB * j), lanes), NN))
            wh[block(n), lanes], wl[block(n), lanes] = a

        def make_ahead():
            n = len(go)
            wh[block(n), :], wl[block(n), :] = sh[block(t + 1), :], sl[block(t + 1), :]

        rows = NB * (len(go) + ahead)

        def make_z(lanes, depth, last):
            new = stacked3((wh[:rows, depth], wl[:rows, depth]), (gh[depth, lanes], gl[depth, lanes]), NN)
            part[0] = new if depth.start == 0 else part[0] + new
            if last:
                zh[:rows, lanes], zl[:rows, lanes] = split(part[0])

        work = [functools.partial(make_v, k, j) for k, j in tasks]
        work += [functools.partial(make_w, n, k, j, slice(512 * i, 512 * i + 512))
                 for n, (k, j) in enumerate(go + [task for task in tasks if task not in go]) for i in range(2)]
        if ahead:
            work.append(make_ahead)
        if rows:
            work += [functools.partial(make_z, slice(256 * i, 256 * i + 256), slice(256 * d, 256 * d + 256), d == 3)
                     for i in range(4) for d in range(4)]
        invs = inverse_factors([jnp.concatenate([eye, ds[k]], axis=1) for k, j in tasks], 8, NB, work)
        invs = {k: split(inv[:, :NB]) for (k, j), inv in zip(tasks, invs)}
        for n, (k, j) in enumerate(go):
            yh[k + 1, block(j), :], yl[k + 1, block(j), :] = split(stacked3(invs[k], (zh[block(n), :], zl[block(n), :]), NN))
            if k == 3:
                qh[block(j), :], ql[block(j), :] = split(stacked3(invs[k], (wh[block(n), :], wl[block(n), :]), NN))
        if ahead:
            n = len(go)
            yh[0, block(t + 1), :], yl[0, block(t + 1), :] = zh[block(n), :], zl[block(n), :]
        for k, j in tasks:
            if j < NJ - 1:
                th[k, block(j), :], tl[k, block(j), :] = split(stacked3(invs[k], vaug[k], NN))
            if k == 4:
                n = len(go)
                zf[block(j), :] = stacked3(invs[k], (wh[block(n), :], wl[block(n), :]), NN).astype(BF16)

    coef = zf[...]
    for part in range(4):
        here = pl.ds(32 * part, 32)
        xs = jnp.concatenate([b_ref[0, 5, 0, here, :], b_ref[0, 5, 1, here, :]], axis=1).astype(BF16)
        term = dot(xs, coef[:, 256 * part:256 * (part + 1)], NT)
        panel = term if part == 0 else panel + term
    ph = split(panel)
    small = jnp.concatenate(
        [eye[:32, :32], dot3(ph, ph, NT), jnp.zeros((32, 64), F32)], axis=1)

    load.wait()
    stores = []
    for n in range(8):
        here = pl.ds(256 * n, 256)
        basis = dot(x_ref[here, :], coef, NT)
        basis_ref[here, :] = basis
        modes_ref[here, :] = basis.astype(BF16)
        stores.append(pltpu.make_async_copy(modes_ref.at[here, :], modes_hbm.at[here, :], modes_sem.at[n]))
        stores[-1].start()

    inv = split(inverse_factors([small], 4, 32)[0][:, :32])
    pbt = dot3(inv, ph, NN)
    pb_ref[...] = pbt
    pb = split(pbt.T)
    proj = split(dot3(pb, pb, NT))
    ones = jnp.ones((8, 256), BF16)
    for n in range(8):
        here = pl.ds(256 * n, 256)
        basis = basis_ref[here, :]
        remaining = basis - dot3(split(basis), proj, NN)
        hi, lo = split(remaining * remaining)
        total = dot(ones, hi, NT) + dot(ones, lo, NT)
        scores_ref[2 * n:2 * n + 1, :] = total[:1, :128] * (1.0 / 256)
        scores_ref[2 * n + 1:2 * n + 2, :] = total[:1, 128:] * (1.0 / 256)
    for copy in stores:
        copy.wait()


def iterate_call(packed, start, x, inv_rows):
    vmem = lambda: pl.BlockSpec(memory_space=pltpu.VMEM)
    hbm = lambda: pl.BlockSpec(memory_space=pltpu.HBM)
    rows = x.shape[0]
    return pl.pallas_call(
        functools.partial(iterate_kernel, inv_rows),
        out_shape=(jax.ShapeDtypeStruct((rows, 256), BF16), jax.ShapeDtypeStruct((rows // 128, 128), F32),
                   jax.ShapeDtypeStruct((32, 256), F32)),
        in_specs=[vmem(), vmem(), hbm()],
        out_specs=(hbm(), vmem(), vmem()),
        scratch_shapes=[
            pltpu.VMEM((1024, 1024), BF16), pltpu.VMEM((1024, 1024), BF16),
            pltpu.VMEM((256, 1024), BF16), pltpu.VMEM((256, 1024), BF16),
            pltpu.VMEM((5, 256, 1024), BF16), pltpu.VMEM((5, 256, 1024), BF16),
            pltpu.VMEM((256, 1024), BF16), pltpu.VMEM((256, 1024), BF16),
            pltpu.VMEM((5, 256, 256), BF16), pltpu.VMEM((5, 256, 256), BF16),
            pltpu.VMEM((256, 1024), BF16), pltpu.VMEM((256, 1024), BF16),
            pltpu.VMEM((256, 1024), BF16), pltpu.VMEM((256, 1024), BF16),
            pltpu.VMEM((256, 1024), BF16),
            pltpu.VMEM((rows, 1024), BF16), pltpu.VMEM((rows, 256), BF16), pltpu.VMEM((rows, 256), F32),
            pltpu.SemaphoreType.DMA, pltpu.SemaphoreType.DMA((8,)),
        ],
        compiler_params=pltpu.CompilerParams(vmem_limit_bytes=50 * 1024 * 1024),
        name="iterate",
    )(packed, start, x)


def local(snapshots, start, pivot_dev, pivot_row):
    rows_total = snapshots.shape[0] * lax.axis_size(AXES)
    packed = reduce_call(snapshots, pivot_dev, pivot_row)
    modes, scores, panel_basis = iterate_call(packed.reshape(2, 6, 2, 256, 128), start, snapshots, 1.0 / rows_total)
    return (modes, scores.reshape(-1), panel_basis.T)


def solution(mesh):
    torus = Mesh(mesh.devices.reshape(4, 4, 4, 2), AXES)
    rows = ("y", "core", "x", "z")
    return jax.shard_map(
        local,
        mesh=torus,
        in_specs=(P(rows, None), P(), P(), P()),
        out_specs=(P(rows, None), P(rows), P()),
        check_vma=False,
    )
```
